256 devices in a mesh: context: 16 (over x_lo, y, core), tensor: 16 (over z, x_hi).
Axes of the slice: x: 4 (x_hi: 2, x_lo: 2; x = x_hi * 2 + x_lo), y: 4, z: 8, core: 2. Of those that a mesh axis runs over, the one named last changes fastest.
Arguments:
- ids: int32 [16384], P('context'), may hold values from 0 to 4, as said below
- complement: int32 [5], replicated, may hold values from 0 to 4, as said below
- embedding: bfloat16 [5, 2048], replicated, may hold values from -6 to 6
- norm_gain: float32 [2048], replicated, may hold values from 0.5 to 1.5
- w_z: bfloat16 [2048, 4096], P(None, 'tensor'), may hold values from -0.125 to 0.125
- w_x: bfloat16 [2048, 4096], P(None, 'tensor'), may hold values from -0.125 to 0.125
- w_bc: bfloat16 [2048, 256], replicated, may hold values from -0.125 to 0.125
- w_dt: bfloat16 [2048, 64], P(None, 'tensor'), may hold values from -0.0625 to 0.0625
- dt_bias: float32 [64], P('tensor')
- a_log: float32 [64], P('tensor')
- conv_x: float32 [4, 4096], P(None, 'tensor'), may hold values from -3 to 3
- conv_bc: float32 [4, 256], replicated, may hold values from -3 to 3
- d_skip: float32 [64], P('tensor'), may hold values from 0.5 to 2
- gate_gain: float32 [4096], P('tensor'), may hold values from 0.5 to 1.5
- w_out: bfloat16 [4096, 2048], P('tensor'), may hold values from -0.09375 to 0.09375
Outputs:
- mixed: bfloat16 [16384, 2048], P('context', 'tensor')
The draws below stay inside these ranges and needn't reach their ends.
Inputs may be any that keep to these rules, and one draw needn't show every extreme that they name: Token ids of the bases and 4 for an unknown base; 4 occurs somewhere in every draw. `complement`: an involution: it pairs the ids 0 to 3 two by two and maps 4 to itself.
All inputs are finite; a program needn't handle non-finite values.
Results may differ from the reference program's by a relative error of at most 0.025.
Values may be sent and summed in bfloat16 or wider, within the bound.
No kernel may reach another device: no remote copies, remote signals or barrier semaphores. Data moves between devices by JAX's collectives and lax.ppermute only.
A program may use at most 128 MiB of HBM per device.

```python
import math
import jax
import jax.numpy as jnp
from jax import lax

D = 2048
HEADS = 64
HEAD = 64
STATE = 128
CONV = 4
BLOCK = 256
INNER = 4096
SEQ = 16384


def head_plan(key, slow_share):
    key_step, key_slow, key_keep, key_fast = jax.random.split(key, 4)
    base_step = jnp.exp(jax.random.uniform(key_step, (HEADS,), jnp.float32, math.log(0.01), math.log(0.1)))
    slow_heads = jax.random.uniform(key_slow, (HEADS,), jnp.float32) < slow_share
    slow_rate = 0.3 / SEQ * jnp.exp(jax.random.uniform(key_keep, (HEADS,), jnp.float32, -0.5, 0.5))
    fast_rate = jnp.exp(-jax.random.uniform(key_fast, (HEADS,), jnp.float32, math.log(30.0), math.log(50.0)))
    per_step = jnp.where(slow_heads, slow_rate, fast_rate)
    return (base_step, per_step / base_step)


def draw_a_log(key, part):
    slow_share = 0.5
    base_step, decay_rate = head_plan(key, slow_share)
    return jnp.log(decay_rate)


def draw_dt_bias(key, part):
    slow_share = 0.5
    base_step, decay_rate = head_plan(key, slow_share)
    return jnp.log(jnp.expm1(base_step))


def draw_ids(key, part):
    key = jax.random.fold_in(key, 3)
    key_base, key_rare, key_spot = jax.random.split(key, 3)
    bases = jax.random.randint(key_base, (SEQ,), 0, 4)
    unknown = jax.random.randint(key_rare, (SEQ,), 0, max(SEQ // 4, 1))
    marked = jnp.where(unknown == 0, 4, bases)
    position = jax.random.randint(key_spot, (), 0, SEQ)
    return marked.at[position].set(4).astype(jnp.int32)


def draw_complement(key, part):
    key = jax.random.fold_in(key, 5)
    order = jax.random.permutation(key, 4).astype(jnp.int32)
    table = jnp.full((5,), 4, jnp.int32)
    table = table.at[order[0]].set(order[1]).at[order[1]].set(order[0])
    table = table.at[order[2]].set(order[3]).at[order[3]].set(order[2])
    return table


def steps_of(rng, shape, cuts, low, top_value):
    def one(dim, parts):
        draws = jax.random.uniform(jax.random.fold_in(jax.random.fold_in(rng, 6), dim), (parts,), jnp.float32, low / len(cuts), top_value / len(cuts))
        return jnp.repeat(jnp.exp(draws), shape[dim] // parts).reshape((-1,) + (1,) * (len(shape) - dim - 1))

    level = one(*cuts[0])
    for cut in cuts[1:]:
        level = level * one(*cut)
    return level


def noise(key, shape, spread, reach, cuts=(), held_as=jnp.bfloat16):
    factor_of = steps_of(key, shape, cuts, -0.22, 0.18) if cuts else 1.0
    entries = jax.random.normal(key, shape, jnp.float32) * spread * factor_of
    return jnp.minimum(jnp.maximum(entries, -reach), reach).astype(held_as)


def setup_inputs(seed: int = 0) -> dict:
    keys = jax.random.split(jax.random.key(seed), 16)
    return {
        "ids": draw_ids(jax.random.fold_in(keys[15], 71), 0),
        "complement": draw_complement(jax.random.fold_in(keys[15], 71), 0),
        "embedding": noise(keys[2], (5, D), 1.0, 6.0),
        "norm_gain": jnp.clip(1.0 + 0.1 * jax.random.normal(keys[3], (D,), jnp.float32), 0.5, 1.5),
        "w_z": noise(keys[4], (D, INNER), D ** -0.5, 0.125, ((1, 16),)),
        "w_x": noise(keys[5], (D, INNER), D ** -0.5, 0.125, ((1, 16),)),
        "w_bc": noise(keys[6], (D, 2 * STATE), D ** -0.5, 0.125),
        "w_dt": noise(keys[7], (D, HEADS), (4 * D) ** -0.5, 0.0625, ((1, 16),)),
        "dt_bias": draw_dt_bias(jax.random.fold_in(keys[15], 71), 0),
        "a_log": draw_a_log(jax.random.fold_in(keys[15], 71), 0),
        "conv_x": noise(keys[10], (CONV, INNER), CONV ** -0.5, 3.0, ((1, 16),), jnp.float32),
        "conv_bc": noise(keys[11], (CONV, 2 * STATE), CONV ** -0.5, 3.0, (), jnp.float32),
        "d_skip": jnp.clip(0.5 + 1.5 * jax.random.uniform(keys[12], (HEADS,), jnp.float32) ** steps_of(keys[12], (HEADS,), ((0, 16),), -0.2, 0.2), 0.5, 2.0),
        "gate_gain": jnp.clip(1.0 + 0.1 * jax.random.normal(keys[13], (INNER,), jnp.float32), 0.5, 1.5),
        "w_out": noise(keys[14], (INNER, D), INNER ** -0.5, 0.09375, ((0, 16),)),
    }


highest = lax.Precision.HIGHEST
epsilon = 1e-05

def causal_conv(values, kernel):
    padded = jnp.concatenate([jnp.zeros((CONV - 1, values.shape[1]), jnp.float32), values.astype(jnp.float32)], axis=0)
    result = kernel[0] * padded[0:SEQ]
    for offset in range(1, CONV):
        result = result + kernel[offset] * padded[offset:offset + SEQ]
    return result

def state_space(values, steps, rates, inputs, readout):
    count = SEQ // BLOCK
    lower = jnp.arange(BLOCK)[:, None] >= jnp.arange(BLOCK)[None, :]

    def advance(state, piece):
        vals, stride, feed, reader = piece
        cumul = jnp.cumsum(stride * rates[None, :], axis=0)
        differ = cumul[:, None, :] - cumul[None, :, :]
        decays = jnp.exp(jnp.where(lower[:, :, None], differ, -jnp.inf))
        scores = jnp.dot(reader, feed.T, precision=highest)
        weights = decays * scores[:, :, None] * stride[None, :, :]
        inside = jnp.einsum('tsh,shp->thp', weights, vals, precision=highest)
        carried = jnp.einsum('tn,hpn->thp', reader, state, precision=highest) * jnp.exp(cumul)[:, :, None]
        remain = jnp.exp(cumul[-1][None, :] - cumul) * stride
        update = jnp.einsum('shp,sn->hpn', vals * remain[:, :, None], feed, precision=highest)
        state = jnp.exp(cumul[-1])[:, None, None] * state + update
        return (state, inside + carried)
    pieces = (values.reshape(count, BLOCK, HEADS, HEAD), steps.reshape(count, BLOCK, HEADS), inputs.reshape(count, BLOCK, STATE), readout.reshape(count, BLOCK, STATE))
    final_state, outputs = lax.scan(advance, jnp.zeros((HEADS, HEAD, STATE), jnp.float32), pieces)
    return outputs.reshape(SEQ, HEADS, HEAD)

def strand(tokens, embedding, norm_gain, w_z, w_x, w_bc, w_dt, dt_bias, a_log, conv_x, conv_bc, d_skip, gate_gain, w_out):
    embedded = embedding[tokens].astype(jnp.float32)
    normed = (embedded * lax.rsqrt(lax.optimization_barrier(jnp.mean(embedded * embedded, axis=-1, keepdims=True)) + epsilon) * norm_gain).astype(jnp.bfloat16)
    gate_in = jnp.dot(normed, w_z, preferred_element_type=jnp.float32).astype(jnp.bfloat16)
    xs_pre = jnp.dot(normed, w_x, preferred_element_type=jnp.float32).astype(jnp.bfloat16)
    bc_pre = jnp.dot(normed, w_bc, preferred_element_type=jnp.float32).astype(jnp.bfloat16)
    stride = jax.nn.softplus(jnp.dot(normed, w_dt, preferred_element_type=jnp.float32) + dt_bias)
    inner_act = jax.nn.silu(causal_conv(xs_pre, conv_x))
    vector_act = jax.nn.silu(causal_conv(bc_pre, conv_bc))
    b_in = vector_act[:, :STATE]
    c_out = vector_act[:, STATE:]
    heads_view = inner_act.reshape(SEQ, HEADS, HEAD)
    scanned = state_space(heads_view, stride, -jnp.exp(a_log), b_in, c_out)
    scanned = scanned + d_skip[None, :, None] * heads_view
    gated = scanned.reshape(SEQ, INNER) * jax.nn.silu(gate_in.astype(jnp.float32))
    normalized = (gated * lax.rsqrt(lax.optimization_barrier(jnp.mean(gated * gated, axis=-1, keepdims=True)) + epsilon) * gate_gain).astype(jnp.bfloat16)
    return jnp.dot(normalized, w_out, preferred_element_type=jnp.float32)

def reference(ids, complement, embedding, norm_gain, w_z, w_x, w_bc, w_dt, dt_bias, a_log, conv_x, conv_bc, d_skip, gate_gain, w_out):
    weights = (embedding, norm_gain, w_z, w_x, w_bc, w_dt, dt_bias, a_log, conv_x, conv_bc, d_skip, gate_gain, w_out)
    forward_out = strand(ids, *weights)
    reverse_ids = complement[ids][::-1]
    reverse_out = strand(reverse_ids, *weights)
    return (forward_out + reverse_out[::-1]).astype(jnp.bfloat16)
```

```python
import functools

import jax
import jax.numpy as jnp
from jax import lax
from jax.experimental import pallas as pl
from jax.experimental.pallas import tpu as pltpu
from jax.sharding import PartitionSpec as P

f32 = jnp.float32
bf16 = jnp.bfloat16
i32 = jnp.int32
highest = lax.Precision.HIGHEST
epsilon = 1e-05

LANES = 128
SEQ = 16384
ROWS = SEQ // LANES
BLOCK = 256
STATE = 128
HEAD = 64
TOKENS = 5
NONE = 5
WIDE = 1024
HEADS = WIDE // HEAD
GRAMS = 144

SAME_HEADS = [[0, 1, 2, 3], [4, 5, 6, 7], [8, 9, 10, 11], [12, 13, 14, 15]]
SAME_POSITIONS = [[0, 4, 8, 12], [1, 5, 9, 13], [2, 6, 10, 14], [3, 7, 11, 15]]

TN = (((0,), (0,)), ((), ()))
NT = (((1,), (1,)), ((), ()))


def iota(shape, dim):
    return lax.broadcasted_iota(i32, shape, dim)


def silu(v):
    return v / (1.0 + jnp.exp(-v))


def split(x, terms=3):
    parts = []
    for _ in range(terms):
        part = x.astype(bf16)
        parts.append(part)
        x = x - part.astype(f32)
    return parts


def table_kernel(
    emb, gain, wz, wx, wbc, wdt, bias, alog, dskip, convx, convbc, ggain, tab, cbc, rows
):
    rows[...] = jnp.zeros_like(rows)
    rows[0:TOKENS, :] = emb[...].astype(f32)
    e = rows[...]
    normed = (
        e * lax.rsqrt(jnp.mean(e * e, axis=-1, keepdims=True) + epsilon) * gain[...]
    ).astype(bf16)

    def project(w):
        return jnp.dot(normed, w[...], preferred_element_type=f32)

    z = project(wz).astype(bf16).astype(f32)
    xs = project(wx).astype(bf16).astype(f32)
    bc = project(wbc).astype(bf16).astype(f32)
    raw = project(wdt) + bias[...]
    dt = jnp.maximum(raw, 0.0) + jnp.log1p(jnp.exp(-jnp.abs(raw)))
    width = z.shape[1]

    def spread(v):
        lane = iota((v.shape[0], width), 1)
        out = jnp.broadcast_to(v[:, 0:1], lane.shape)
        for h in range(1, v.shape[1]):
            out = jnp.where(lane >= h * HEAD, v[:, h : h + 1], out)
        return out

    row = iota((8, width), 0)
    own = jnp.where(row == 6, spread(dskip[...]), spread(jnp.exp(alog[...])))
    own = jnp.where(row == 5, ggain[...], own)
    tab[0:8, :] = jnp.where(row < TOKENS, silu(z), own)
    tab[8:16, :] = xs
    tab[16:24, :] = jnp.zeros((8, width), f32)
    tab[16:20, :] = convx[...]
    tab[24:32, :] = jnp.where(row < TOKENS, spread(dt), 0.0)
    for k in range(4):
        cbc[8 * k : 8 * k + 8, :] = convbc[k : k + 1, :] * bc


def block_kernel(
    place, comp, ids_ref, t0, t1, t2, t3, cbc, vg, sq, toks, gram, side_tok, count
):
    r0 = place[0]
    ids = ids_ref[...]
    row = iota((ROWS, LANES), 0)
    lane = iota((ROWS, LANES), 1)
    at = row * LANES + lane
    flip = jnp.zeros_like(ids)
    for k in range(TOKENS):
        flip = jnp.where(ids == k, comp[k], flip)

    def before(x):
        y = pltpu.roll(x, 1, 1)
        y = jnp.where(lane == 0, pltpu.roll(y, 1, 0), y)
        return jnp.where(at == 0, NONE, y)

    def after(x):
        y = pltpu.roll(x, LANES - 1, 1)
        y = jnp.where(lane == LANES - 1, pltpu.roll(y, ROWS - 1, 0), y)
        return jnp.where(at == SEQ - 1, NONE, y)

    fs = [ids]
    rs = [flip]
    for k in range(3):
        fs.append(before(fs[-1]))
        rs.append(after(rs[-1]))
    for k in range(4):
        toks[k] = fs[k]
        toks[4 + k] = rs[k]
    g_f = 25 * fs[3] + 5 * fs[2] + fs[1]
    g_r = 25 * rs[3] + 5 * rs[2] + rs[1]
    for k in range(3):
        g_f = jnp.where(at == k, 125 + k, g_f)
        g_r = jnp.where(at == SEQ - 1 - k, 125 if k == 0 else 127 + k, g_r)
    ahead = row < r0
    tok = jnp.where(ahead, ids, flip)
    tok = jnp.where(ahead | (row > r0 + 1), tok, -1)
    gram[...] = jnp.where(ahead, g_f, g_r)
    side_tok[...] = tok

    hot = [jnp.where(tok == k, 1.0, 0.0) for k in range(TOKENS)]
    hots = jnp.concatenate(hot, axis=0).astype(bf16)
    strict = jnp.where(row < lane, 1.0, 0.0).astype(bf16)
    prior = jnp.dot(hots, strict, preferred_element_type=f32)
    total = jnp.dot(hots, jnp.ones((LANES, LANES), bf16), preferred_element_type=f32)
    between = ((row < lane) & (lane < r0)) | ((lane > r0 + 1) & (lane < row))
    between = jnp.where(between, 1.0, 0.0).astype(bf16)
    for k in range(TOKENS):
        part = slice(k * ROWS, (k + 1) * ROWS)
        far = jnp.dot(between, total[part].astype(bf16), preferred_element_type=f32)
        near = jnp.where(ahead, total[part] - prior[part] - hot[k], prior[part])
        count[k] = near + far

    tab = jnp.concatenate([t0[...], t1[...], t2[...], t3[...]], axis=1)
    dt_tab = tab[24:32]
    rate_tab = tab[7:8] * dt_tab
    pick = jnp.where(iota((HEADS, WIDE), 1) == HEAD * iota((HEADS, WIDE), 0), 1.0, 0.0)
    rate = lax.dot_general(pick, rate_tab, NT, precision=highest, preferred_element_type=f32)
    rate_t = lax.dot_general(rate_tab, pick, NT, precision=highest, preferred_element_type=f32)
    columns = [jnp.broadcast_to(-rate[:, k : k + 1], (HEADS, BLOCK)) for k in range(TOKENS)]

    def pair(ref, index):
        r = 2 * index
        return jnp.concatenate([ref[pl.ds(r, 1), :], ref[pl.ds(r + 1, 1), :]], axis=1)

    gram_row = iota((GRAMS, BLOCK), 0)

    def gather(step, total):
        windows = []
        weights = []
        for j in range(4):
            index = 4 * step + j
            token = pair(side_tok, index)
            window = pair(gram, index)
            exponent = columns[0] * pair(count.at[0], index)
            for k in range(1, TOKENS):
                exponent = exponent + columns[k] * pair(count.at[k], index)
            weight = jnp.exp(exponent)
            first = jnp.where(2 * index < r0, 1.0, 0.0)
            forward = weight * first
            reverse = weight * (1.0 - first)
            weights.append(
                jnp.concatenate(
                    [
                        jnp.where(token == k, w, 0.0)
                        for w in (forward, reverse)
                        for k in range(TOKENS)
                    ],
                    axis=0,
                ).astype(bf16)
            )
            windows.append(jnp.where(gram_row == window, 1.0, 0.0).astype(bf16))
        return total + lax.dot_general(
            jnp.concatenate(windows, axis=1),
            jnp.concatenate(weights, axis=1),
            NT,
            preferred_element_type=f32,
        )

    hist = jnp.zeros((GRAMS, 2 * TOKENS * HEADS), f32)
    for step in range(ROWS // 8):
        hist = gather(step, hist)
    hist = hist.astype(bf16)

    taps = jnp.concatenate([tab[16 + k : 17 + k] * tab[8:16] for k in range(4)], axis=0)
    bc_taps = cbc[...]
    g = iota((GRAMS, 24), 0)
    col = iota((GRAMS, 24), 1)
    d0 = sum(jnp.where(g >= 25 * m, 1, 0) for m in range(1, TOKENS))
    rest = g - 25 * d0
    d1 = sum(jnp.where(rest >= 5 * m, 1, 0) for m in range(1, TOKENS))
    d2 = rest - 5 * d1
    plain = g < 125
    d0 = jnp.where(plain, d0, NONE)
    d1 = jnp.where(plain, d1, NONE)
    d2 = jnp.where(plain, d2, NONE)
    d1 = jnp.where(g == 127, ids[0:1, 0:1], d1)
    d2 = jnp.where(g == 126, ids[0:1, 0:1], d2)
    d2 = jnp.where(g == 127, ids[0:1, 1:2], d2)
    d1 = jnp.where(g == 129, flip[ROWS - 1 :, LANES - 1 :], d1)
    d2 = jnp.where(g == 128, flip[ROWS - 1 :, LANES - 1 :], d2)
    d2 = jnp.where(g == 129, flip[ROWS - 1 :, LANES - 2 : LANES - 1], d2)
    digit = jnp.where(col < 8, d0, jnp.where(col < 16, d1, d2))
    older = jnp.where(digit == (col & 7), 1.0, 0.0)
    x_older = jnp.dot(older, taps[0:24], precision=highest, preferred_element_type=f32)
    b_older = jnp.dot(older, bc_taps[0:24, :STATE], precision=highest, preferred_element_type=f32)
    lift = iota((HEADS, WIDE), 1) - HEAD * iota((HEADS, WIDE), 0)
    lift = jnp.where((lift >= 0) & (lift < HEAD), 1.0, 0.0).astype(bf16)
    feeds = []
    moved = [[], []]
    for k in range(TOKENS):
        feeds.append(silu(b_older + bc_taps[24 + k : 25 + k, :STATE]).astype(bf16))
        act = silu(x_older + taps[24 + k : 25 + k]) * dt_tab[k : k + 1]
        for s in range(2):
            start = (s * TOKENS + k) * HEADS
            part = jnp.dot(hist[:, start : start + HEADS], lift, preferred_element_type=f32)
            moved[s].append((act * part).astype(bf16))
    feeds = jnp.concatenate(feeds, axis=0)
    entering = [
        lax.dot_general(
            feeds, jnp.concatenate(moved[s], axis=0), TN, preferred_element_type=f32
        ).astype(bf16)
        for s in range(2)
    ]

    def own(m):
        return jnp.concatenate([toks[m, pl.ds(r0, 1), :], toks[m, pl.ds(r0 + 1, 1), :]], axis=1)

    place_row = iota((32, BLOCK), 0)
    hot_own = []
    for s in range(2):
        digit = own(4 * s)
        for k in range(3):
            digit = jnp.where(place_row < 8 * (3 - k), own(4 * s + k + 1), digit)
        hot_own.append(jnp.where(digit == (place_row & 7), 1.0, 0.0))
    hot_all = jnp.concatenate(hot_own, axis=1)
    hot_taps = jnp.concatenate([hot_all] * 3, axis=0).astype(bf16)
    hot_now = jnp.concatenate([hot_all[24:32]] * 3, axis=0).astype(bf16)

    def look(hots, table):
        return lax.dot_general(
            hots, jnp.concatenate(split(table), axis=0), TN, preferred_element_type=f32
        )

    bc_act = silu(look(hot_taps, bc_taps))
    lane_b = iota((BLOCK, BLOCK), 1)
    row_b = iota((BLOCK, BLOCK), 0)
    lane_p = iota((BLOCK, LANES), 1)
    low = lane_p < HEAD
    gate_tab = jnp.where(iota((8, WIDE), 0) < TOKENS, tab[0:8], 0.0)
    for s in range(2):
        rows = slice(s * BLOCK, (s + 1) * BLOCK)
        taps_s = hot_taps[:, rows]
        now_s = hot_now[:, rows]
        feed = bc_act[rows, :STATE].astype(bf16)
        read = bc_act[rows, STATE:].astype(bf16)
        seen = (lane_b <= row_b) if s == 0 else (lane_b >= row_b)
        scores = lax.dot_general(read, feed, NT, preferred_element_type=f32)
        scores = jnp.where(seen, scores, 0.0)
        inclusive = (row_b <= lane_b) if s == 0 else (row_b >= lane_b)
        inclusive = jnp.where(inclusive, 1.0, 0.0).astype(bf16)
        counts = jnp.dot(hot_own[s][24:32].astype(bf16), inclusive, preferred_element_type=f32)
        cum_row = -jnp.dot(rate, counts, precision=highest, preferred_element_type=f32)
        cum_col = -lax.dot_general(
            counts, rate_t, TN, precision=highest, preferred_element_type=f32
        )
        decay = jnp.exp(cum_col)
        squares = jnp.zeros((BLOCK, LANES), f32)
        for p in range(HEADS // 2):
            chans = slice(p * LANES, (p + 1) * LANES)
            xs = silu(look(taps_s, taps[:, chans]))
            steps = look(now_s, dt_tab[:, chans])
            gate = look(now_s, gate_tab[:, chans])
            fed = (xs * steps).astype(bf16)
            parts = []
            for h in (2 * p, 2 * p + 1):
                differ = cum_col[:, h : h + 1] - cum_row[h : h + 1, :]
                parts.append((jnp.exp(jnp.minimum(differ, 0.0)) * scores).astype(bf16))
            zero = jnp.zeros_like(fed)
            inside = jnp.dot(
                jnp.concatenate(parts, axis=1),
                jnp.concatenate([jnp.where(low, fed, zero), jnp.where(low, zero, fed)], axis=0),
                preferred_element_type=f32,
            )
            carried = jnp.dot(read, entering[s][:, chans], preferred_element_type=f32)
            carried = carried * jnp.where(
                low, decay[:, 2 * p : 2 * p + 1], decay[:, 2 * p + 1 : 2 * p + 2]
            )
            v = (inside + carried + tab[6:7, chans] * xs) * gate
            squares = squares + v * v
            vg[rows, chans] = (v * tab[5:6, chans]).astype(bf16)
        summed = lax.dot_general(
            jnp.ones((8, LANES), f32), squares, NT, precision=highest, preferred_element_type=f32
        )
        sq[:, rows] = summed[0:1]


def out_kernel(parity, vg, sq, w_own, a1, a2, a3, b1, b2, b3, out, g_all):
    @pl.when(pl.program_id(0) == 0)
    def _():
        first = iota((8, 2 * BLOCK), 0) == 0
        inverse = jnp.where(first, lax.rsqrt(sq[...] / 4096.0 + epsilon), 0.0)
        inverse = lax.dot_general(
            inverse, jnp.ones((8, LANES), f32), TN, precision=highest, preferred_element_type=f32
        )
        for p in range(WIDE // LANES):
            chans = slice(p * LANES, (p + 1) * LANES)
            strands = [
                (vg[s * BLOCK : (s + 1) * BLOCK, chans].astype(f32) * inverse[s * BLOCK : (s + 1) * BLOCK])
                .astype(bf16)
                .astype(f32)
                for s in range(2)
            ]
            g_all[:, chans] = (strands[0] + strands[1]).astype(bf16)

    even = parity[0] == 0
    weights = [w_own[...]]
    for a, b in ((a1, b1), (a2, b2), (a3, b3)):
        mine = a[...]
        theirs = b[...]
        weights.append(jnp.where(even, mine, theirs))
        weights.append(jnp.where(even, theirs, mine))
    result = jnp.dot(
        g_all[...], jnp.concatenate(weights, axis=0), preferred_element_type=f32
    ).astype(bf16)
    for j in range(out.shape[0]):
        out[j] = result[:, j * LANES : (j + 1) * LANES]


def build_tables(
    embedding, norm_gain, w_z, w_x, w_bc, w_dt, dt_bias, a_log, d_skip, conv_x, conv_bc, gate_gain
):
    width = w_z.shape[1]
    return pl.pallas_call(
        table_kernel,
        out_shape=(
            jax.ShapeDtypeStruct((32, width), f32),
            jax.ShapeDtypeStruct((32, w_bc.shape[1]), f32),
        ),
        scratch_shapes=[pltpu.VMEM((8, embedding.shape[1]), f32)],
        compiler_params=pltpu.CompilerParams(vmem_limit_bytes=40 * 2**20),
        name="tables",
    )(
        embedding,
        norm_gain[None],
        w_z,
        w_x,
        w_bc,
        w_dt,
        dt_bias[None],
        a_log[None],
        d_skip[None],
        conv_x,
        conv_bc,
        gate_gain[None],
    )


def run_block(place, complement, ids, tabs, cbc):
    smem = pl.BlockSpec(memory_space=pltpu.SMEM)
    vmem = pl.BlockSpec(memory_space=pltpu.VMEM)
    return pl.pallas_call(
        block_kernel,
        in_specs=[smem, smem] + [vmem] * 6,
        out_specs=(vmem, vmem),
        out_shape=(
            jax.ShapeDtypeStruct((2 * BLOCK, WIDE), bf16),
            jax.ShapeDtypeStruct((1, 2 * BLOCK), f32),
        ),
        scratch_shapes=[
            pltpu.VMEM((8, ROWS, LANES), i32),
            pltpu.VMEM((ROWS, LANES), i32),
            pltpu.VMEM((ROWS, LANES), i32),
            pltpu.VMEM((TOKENS, ROWS, LANES), f32),
        ],
        compiler_params=pltpu.CompilerParams(vmem_limit_bytes=48 * 2**20),
        name="block",
    )(place, complement, ids, *tabs, cbc)


def run_out(parity, vg, sq, w_own, mine, theirs):
    features = w_own.shape[1]
    tile = 512
    half = w_own.shape[0] // 2
    whole = pl.BlockSpec((2 * BLOCK, WIDE), lambda n: (0, 0))
    half_spec = pl.BlockSpec((half, tile), lambda n: (0, n))
    return pl.pallas_call(
        out_kernel,
        grid=(features // tile,),
        in_specs=[
            pl.BlockSpec(memory_space=pltpu.SMEM),
            whole,
            pl.BlockSpec((1, 2 * BLOCK), lambda n: (0, 0)),
            pl.BlockSpec((2 * half, tile), lambda n: (0, n)),
        ]
        + [half_spec] * 6,
        out_specs=pl.BlockSpec((tile // LANES, BLOCK, LANES), lambda n: (n, 0, 0)),
        out_shape=jax.ShapeDtypeStruct((features // LANES, BLOCK, LANES), bf16),
        scratch_shapes=[pltpu.VMEM((BLOCK, WIDE), bf16)],
        compiler_params=pltpu.CompilerParams(vmem_limit_bytes=40 * 2**20),
        name="project",
    )(parity, vg, sq, w_own, *mine, *theirs)


def swap(x, axis, distance):
    count = lax.axis_size(axis)
    return lax.ppermute(x, axis, [(i, i ^ distance) for i in range(count)])


def local(
    ids,
    complement,
    embedding,
    norm_gain,
    w_z,
    w_x,
    w_bc,
    w_dt,
    dt_bias,
    a_log,
    conv_x,
    conv_bc,
    d_skip,
    gate_gain,
    w_out,
):
    context = lax.axis_index("context").astype(i32)
    tensor = lax.axis_index("tensor").astype(i32)
    parity = context % 2
    half = w_out.shape[0] // 2
    share = lax.dynamic_slice_in_dim(w_out, parity * half, half, 0)
    mine = [swap(share, "tensor", d) for d in (1, 2, 3)]
    theirs = [swap(x, "context", 1) for x in mine]

    tab, cbc = build_tables(
        embedding, norm_gain, w_z, w_x, w_bc, w_dt, dt_bias, a_log, d_skip, conv_x, conv_bc, gate_gain
    )
    tabs = [tab] + [swap(tab, "tensor", d) for d in (1, 2, 3)]

    count = lax.axis_size("context")
    spread = jnp.broadcast_to(ids.reshape(1, -1, LANES), (count, ids.shape[0] // LANES, LANES))
    everyone = lax.all_to_all(spread, "context", 0, 0, tiled=True).reshape(ROWS, LANES)

    place = (context * (ids.shape[0] // LANES) + (tensor % 4) * (BLOCK // LANES)).reshape(1)
    vg, sq = run_block(place, complement, everyone, tabs, cbc)
    sq = lax.psum(sq, "tensor", axis_index_groups=SAME_POSITIONS)
    terms = run_out(parity.reshape(1), vg, sq, w_out, mine, theirs)
    arrived = lax.all_to_all(terms, "tensor", 0, 0, tiled=True)
    summed = jnp.sum(arrived.astype(f32).reshape(4, 4, BLOCK, LANES), axis=0)
    return summed.reshape(4 * BLOCK, LANES).astype(bf16)


def solution(mesh):
    placed = (
        P("context"),
        P(),
        P(),
        P(),
        P(None, "tensor"),
        P(None, "tensor"),
        P(),
        P(None, "tensor"),
        P("tensor"),
        P("tensor"),
        P(None, "tensor"),
        P(),
        P("tensor"),
        P("tensor"),
        P("tensor", None),
    )
    return jax.shard_map(
        local, mesh=mesh, in_specs=placed, out_specs=P("context", "tensor"), check_vma=False
    )
```

```python
import functools

import jax
import jax.numpy as jnp
from jax import lax
from jax.experimental import pallas as pl
from jax.experimental.pallas import tpu as pltpu
from jax.sharding import PartitionSpec as P

f32 = jnp.float32
bf16 = jnp.bfloat16
i32 = jnp.int32
highest = lax.Precision.HIGHEST
epsilon = 1e-05

LANES = 128
SEQ = 16384
ROWS = SEQ // LANES
BLOCK = 256
STATE = 128
HEAD = 64
TOKENS = 5
NONE = 5
LOG2E = 1.4426950408889634
TINY = 2.0**-126
WIDE = 1024
HEADS = WIDE // HEAD
GRAMS = 144
TABLE_ARGS = 12
PIECES = 4

SAME_HEADS = [[0, 1, 2, 3], [4, 5, 6, 7], [8, 9, 10, 11], [12, 13, 14, 15]]
SAME_POSITIONS = [[0, 4, 8, 12], [1, 5, 9, 13], [2, 6, 10, 14], [3, 7, 11, 15]]

TN = (((0,), (0,)), ((), ()))
NT = (((1,), (1,)), ((), ()))


def iota(shape, dim):
    return lax.broadcasted_iota(i32, shape, dim)


def silu(v):
    half = 0.5 * v
    return half + half * jnp.tanh(half)


def split(x, terms=3):
    parts = []
    for _ in range(terms):
        part = x.astype(bf16)
        parts.append(part)
        x = x - part.astype(f32)
    return parts


def table_kernel(parity, w_out, *refs):
    given = refs[:TABLE_ARGS]
    tab, cbc, share, rows = refs[TABLE_ARGS : TABLE_ARGS + 4]
    held = refs[TABLE_ARGS + 4 : -2]
    arrived, shared = refs[-2:]
    half = share.shape[0]
    part = w_out.at[pl.ds(pl.multiple_of(parity[0] * half, half), half), :]
    copies = []
    for source, target in zip(given, held):
        count = PIECES if source.shape[0] > 1024 else 1
        size = source.shape[0] // count
        for n in range(count):
            span = pl.ds(n * size, size)
            one = (source, target) if count == 1 else (source.at[span, :], target.at[span, :])
            copies.append(pltpu.make_async_copy(*one, arrived.at[len(copies)]))
    for copy in copies:
        copy.start()
    kept = pltpu.make_async_copy(part, share, shared)
    kept.start()
    for copy in copies:
        copy.wait()
    emb, gain, wz, wx, wbc, wdt, bias, alog, dskip, convx, convbc, ggain = held
    rows[...] = jnp.zeros_like(rows)
    rows[0:TOKENS, :] = emb[...].astype(f32)
    e = rows[...]
    normed = (
        e * lax.rsqrt(jnp.mean(e * e, axis=-1, keepdims=True) + epsilon) * gain[...]
    ).astype(bf16)

    def project(w):
        return jnp.dot(normed, w[...], preferred_element_type=f32)

    z = project(wz).astype(bf16).astype(f32)
    xs = project(wx).astype(bf16).astype(f32)
    bc = project(wbc).astype(bf16).astype(f32)
    raw = lax.dot_general(normed, wdt[...], NT, preferred_element_type=f32) + bias[...]
    dt = jnp.maximum(raw, 0.0) + jnp.log1p(jnp.exp(-jnp.abs(raw)))
    width = z.shape[1]

    def spread(v):
        lane = iota((v.shape[0], width), 1)
        out = jnp.broadcast_to(v[:, 0:1], lane.shape)
        for h in range(1, v.shape[1]):
            out = jnp.where(lane >= h * HEAD, v[:, h : h + 1], out)
        return out

    row = iota((8, width), 0)
    own = jnp.where(row == 6, spread(dskip[...]), spread(jnp.exp(alog[...])))
    own = jnp.where(row == 5, ggain[...], own)
    tab[0:8, :] = jnp.where(row < TOKENS, silu(z), own)
    tab[8:16, :] = xs
    tab[16:24, :] = jnp.zeros((8, width), f32)
    tab[16:20, :] = convx[...]
    tab[24:32, :] = jnp.where(row < TOKENS, spread(dt), 0.0)
    for k in range(4):
        cbc[8 * k : 8 * k + 8, :] = convbc[k : k + 1, :] * bc
    kept.wait()


def prepare_kernel(
    place, comp, ids_ref, grams, side_tok, count, hot_taps, own_rows, older
):
    r0 = place[0]
    ids = ids_ref[...]
    row = iota((ROWS, LANES), 0)
    lane = iota((ROWS, LANES), 1)
    at = row * LANES + lane
    flip = jnp.zeros_like(ids)
    for k in range(TOKENS):
        flip = jnp.where(ids == k, comp[k], flip)

    def before(x):
        y = pltpu.roll(x, 1, 1)
        y = jnp.where(lane == 0, pltpu.roll(y, 1, 0), y)
        return jnp.where(at == 0, NONE, y)

    def after(x):
        y = pltpu.roll(x, LANES - 1, 1)
        y = jnp.where(lane == LANES - 1, pltpu.roll(y, ROWS - 1, 0), y)
        return jnp.where(at == SEQ - 1, NONE, y)

    fs = [ids]
    rs = [flip]
    for k in range(3):
        fs.append(before(fs[-1]))
        rs.append(after(rs[-1]))
    g_f = 25 * fs[3] + 5 * fs[2] + fs[1]
    g_r = 25 * rs[3] + 5 * rs[2] + rs[1]
    for k in range(3):
        g_f = jnp.where(at == k, 125 + k, g_f)
        g_r = jnp.where(at == SEQ - 1 - k, 125 if k == 0 else 127 + k, g_r)
    ahead = row < r0
    tok = jnp.where(ahead, ids, flip)
    tok = jnp.where(ahead | (row > r0 + 1), tok, -1)
    grams[...] = jnp.where(ahead, g_f, g_r).astype(f32)
    side_tok[...] = tok.astype(f32)

    hot = [jnp.where(tok == k, 1.0, 0.0) for k in range(TOKENS)]
    hots = jnp.concatenate(hot, axis=0).astype(bf16)
    strict = jnp.where(row < lane, 1.0, 0.0).astype(bf16)
    prior = jnp.dot(hots, strict, preferred_element_type=f32)
    total = jnp.dot(hots, jnp.ones((LANES, LANES), bf16), preferred_element_type=f32)
    between = ((row < lane) & (lane < r0)) | ((lane > r0 + 1) & (lane < row))
    between = jnp.where(between, 1.0, 0.0).astype(bf16)
    for k in range(TOKENS):
        part = slice(k * ROWS, (k + 1) * ROWS)
        far = jnp.dot(between, total[part].astype(bf16), preferred_element_type=f32)
        near = jnp.where(ahead, total[part] - prior[part] - hot[k], prior[part])
        count[k] = near + far

    g = iota((GRAMS, LANES), 0)
    col = iota((GRAMS, LANES), 1)
    d0 = sum(jnp.where(g >= 25 * m, 1, 0) for m in range(1, TOKENS))
    rest = g - 25 * d0
    d1 = sum(jnp.where(rest >= 5 * m, 1, 0) for m in range(1, TOKENS))
    d2 = rest - 5 * d1
    plain = g < 125
    d0 = jnp.where(plain, d0, NONE)
    d1 = jnp.where(plain, d1, NONE)
    d2 = jnp.where(plain, d2, NONE)
    d1 = jnp.where(g == 127, ids[0:1, 0:1], d1)
    d2 = jnp.where(g == 126, ids[0:1, 0:1], d2)
    d2 = jnp.where(g == 127, ids[0:1, 1:2], d2)
    d1 = jnp.where(g == 129, flip[ROWS - 1 :, LANES - 1 :], d1)
    d2 = jnp.where(g == 128, flip[ROWS - 1 :, LANES - 1 :], d2)
    d2 = jnp.where(g == 129, flip[ROWS - 1 :, LANES - 2 : LANES - 1], d2)
    tap = (col >> 3) % 3
    digit = jnp.where(tap == 0, d0, jnp.where(tap == 1, d1, d2))
    older[...] = jnp.where((digit == (col & 7)) & (col < 72), 1.0, 0.0).astype(bf16)

    place_row = iota((32, BLOCK), 0)
    lane_b = iota((BLOCK, BLOCK), 1)
    row_b = iota((BLOCK, BLOCK), 0)

    def own(x):
        first = jnp.sum(jnp.where(row == r0, x, 0), axis=0, keepdims=True)
        second = jnp.sum(jnp.where(row == r0 + 1, x, 0), axis=0, keepdims=True)
        return jnp.concatenate([first, second], axis=1)

    for s, values in enumerate((fs, rs)):
        digit = own(values[0])
        for k in range(3):
            digit = jnp.where(place_row < 8 * (3 - k), own(values[k + 1]), digit)
        hot_own = jnp.where(digit == (place_row & 7), 1.0, 0.0)
        now = hot_own[24:32]
        inclusive = (row_b <= lane_b) if s == 0 else (row_b >= lane_b)
        inclusive = jnp.where(inclusive, 1.0, 0.0).astype(bf16)
        counts = jnp.dot(now.astype(bf16), inclusive, preferred_element_type=f32)
        own_rows[16 * s : 16 * s + 8, :] = counts
        own_rows[16 * s + 8 : 16 * s + 16, :] = now
        hot_taps[s * BLOCK : (s + 1) * BLOCK, :] = jnp.concatenate(
            [hot_own] * 2 + [now] * 2 + [counts] * 3 + [jnp.zeros((24, BLOCK), f32)], axis=0
        ).T.astype(bf16)


def block_kernel(
    place, grams, side_tok, count, hot_taps, own_rows, older, t0, t1, t2, t3, cbc, vg, sq
):
    chunk = place[0] // 8
    r0 = place[0]
    tab = jnp.concatenate([t0[...], t1[...], t2[...], t3[...]], axis=1)
    dt_tab = tab[24:32]
    rate_tab = tab[7:8] * dt_tab * LOG2E
    log_tab = jnp.log2(jnp.maximum(dt_tab, TINY))
    pick = jnp.where(iota((HEADS, WIDE), 1) == HEAD * iota((HEADS, WIDE), 0), 1.0, 0.0).astype(bf16)

    def stack(*parts):
        return jnp.concatenate([part.astype(f32) for part in parts], axis=0).astype(bf16)

    spare = jnp.zeros((8, WIDE), f32)
    both_tab = stack(*split(rate_tab), *split(log_tab), spare, spare)
    both = lax.dot_general(pick, both_tab, NT, preferred_element_type=f32)
    rate = both[:, 0:8] + both[:, 8:16] + both[:, 16:24]
    log_dt = both[:, 24:32] + both[:, 32:40] + both[:, 40:48]
    both_t = lax.dot_general(both_tab, pick, NT, preferred_element_type=f32)
    rate_t = both_t[0:8] + both_t[8:16] + both_t[16:24]
    columns = [jnp.broadcast_to(-rate[:, k : k + 1], (HEADS, BLOCK)) for k in range(TOKENS)]

    def pair(ref, r):
        return jnp.concatenate([ref[pl.ds(r, 1), :], ref[pl.ds(r + 1, 1), :]], axis=1)

    nothing = jnp.zeros((HEADS, BLOCK), bf16)

    def weigh(r):
        token = jnp.broadcast_to(pair(side_tok, r), (HEADS, BLOCK)).astype(bf16)
        exponent = columns[0] * pair(count.at[0], r)
        for k in range(1, TOKENS):
            exponent = exponent + columns[k] * pair(count.at[k], r)
        weight = jnp.exp2(exponent)
        return token, weight

    def by_token(token, weight):
        return [jnp.where(token == k, weight, nothing) for k in range(TOKENS)]

    gram_row = iota((GRAMS, BLOCK), 0).astype(bf16)
    one = jnp.ones((GRAMS, BLOCK), bf16)
    none = jnp.zeros((GRAMS, BLOCK), bf16)

    def window(r):
        kind = jnp.broadcast_to(pair(grams, r), (GRAMS, BLOCK)).astype(bf16)
        return jnp.where(gram_row == kind, one, none)

    def tally(seen, weights):
        return lax.dot_general(
            jnp.concatenate(seen, axis=1),
            jnp.concatenate(weights, axis=1),
            NT,
            preferred_element_type=f32,
        )

    sides = [jnp.zeros((GRAMS, TOKENS * HEADS), f32) for _ in range(2)]
    for step in range(ROWS // 8):
        weights = []
        for j in range(4):
            token, weight = weigh(8 * step + 2 * j)
            weights.append(jnp.concatenate(by_token(token, weight.astype(bf16)), axis=0))
        part = tally([window(8 * step + 2 * j) for j in range(4)], weights)
        sides[0] = sides[0] + part * jnp.where(step < chunk, 1.0, 0.0)
        sides[1] = sides[1] + part * jnp.where(step > chunk, 1.0, 0.0)
    weights = []
    for j in range(4):
        r = pl.multiple_of(8 * chunk, 8) + 2 * j
        token, weight = weigh(r)
        first = jnp.where(r < r0, 1.0, 0.0)
        forward = by_token(token, (weight * first).astype(bf16))
        reverse = by_token(token, (weight * (1.0 - first)).astype(bf16))
        weights.append(jnp.concatenate(forward + reverse, axis=0))
    part = tally([window(pl.multiple_of(8 * chunk, 8) + 2 * j) for j in range(4)], weights)
    hist = (part + jnp.concatenate(sides, axis=1)).astype(bf16)

    taps = jnp.concatenate([tab[16 + k : 17 + k] * tab[8:16] for k in range(4)], axis=0)
    bc_taps = cbc[...]
    kinds = older[...]
    rest = jnp.zeros((56, WIDE), f32)
    x_older = jnp.dot(kinds, stack(*split(taps[0:24]), rest), preferred_element_type=f32)
    b_older = jnp.dot(
        kinds, stack(*split(bc_taps[0:24, :STATE]), rest[:, :STATE]), preferred_element_type=f32
    )
    lift = iota((HEADS, WIDE), 1) - HEAD * iota((HEADS, WIDE), 0)
    lift = jnp.where((lift >= 0) & (lift < HEAD), 1.0, 0.0).astype(bf16)
    feeds = []
    moved = [[], []]
    for k in range(TOKENS):
        feeds.append(silu(b_older + bc_taps[24 + k : 25 + k, :STATE]).astype(bf16))
        act = (silu(x_older + taps[24 + k : 25 + k]) * dt_tab[k : k + 1]).astype(bf16)
        for s in range(2):
            start = (s * TOKENS + k) * HEADS
            part = jnp.dot(hist[:, start : start + HEADS], lift, preferred_element_type=f32)
            moved[s].append(act * part.astype(bf16))
    feeds = jnp.concatenate(feeds, axis=0)
    entering = [
        lax.dot_general(
            feeds, jnp.concatenate(moved[s], axis=0), TN, preferred_element_type=f32
        ).astype(bf16)
        for s in range(2)
    ]

    def look(hots, table):
        return jnp.dot(hots, table, preferred_element_type=f32)

    def blank(count, width):
        return jnp.zeros((count, width), f32)

    gate_tab = jnp.where(iota((8, WIDE), 0) < TOKENS, tab[0:8], 0.0)
    taps2 = stack(*split(taps, 2), blank(64, WIDE))
    bc2 = stack(*split(bc_taps, 2), blank(64, 2 * STATE))
    gate2 = stack(blank(64, WIDE), *split(gate_tab, 2), blank(48, WIDE))
    rate3 = stack(blank(80, HEADS), *split(rate_t), blank(24, HEADS))
    cap = jnp.broadcast_to(jnp.max(log_dt[:, :TOKENS], axis=1, keepdims=True), (HEADS, BLOCK))
    row_tab = jnp.concatenate([rate, log_dt], axis=1)
    lane_h = iota((LANES, LANES), 1)
    row_h = iota((LANES, LANES), 0)
    low = iota((BLOCK, LANES), 1) < HEAD
    zero = jnp.zeros((BLOCK, LANES), bf16)
    for s in range(2):
        rows = slice(s * BLOCK, (s + 1) * BLOCK)
        hot = hot_taps[rows, :]
        bc_act = silu(look(hot, bc2))
        feed = bc_act[:, :STATE].astype(bf16)
        read = bc_act[:, STATE:].astype(bf16)
        scores = lax.dot_general(read, feed, NT, preferred_element_type=f32)
        cum_row = -jnp.dot(
            row_tab, own_rows[16 * s : 16 * s + 16, :], precision=highest, preferred_element_type=f32
        )
        cum_col = -look(hot, rate3)
        decay = jnp.exp2(cum_col)
        near = (lane_h <= row_h) if s == 0 else (lane_h >= row_h)
        halves = ((0, 0, 1), (1, 0, 2)) if s == 0 else ((0, 0, 2), (1, 1, 1))
        masked = []
        for half, key, keys in halves:
            t = slice(half * LANES, (half + 1) * LANES)
            pieces = []
            for j in range(key, key + keys):
                piece = scores[t, j * LANES : (j + 1) * LANES]
                pieces.append(jnp.where(near, piece, 0.0) if j == half else piece)
            masked.append(jnp.concatenate(pieces, axis=1).astype(bf16))
        squares = [jnp.zeros((LANES, LANES), f32) for _ in range(2)]
        for p in range(HEADS // 2):
            chans = slice(p * LANES, (p + 1) * LANES)
            if p % 2 == 0:
                wide = slice(p * LANES, (p + 2) * LANES)
                xs_wide = silu(look(hot, taps2[:, wide]))
                gate_wide = look(hot, gate2[:, wide])
                far_wide = look(read, entering[s][:, wide])
            part = slice((p % 2) * LANES, (p % 2 + 1) * LANES)
            xs = xs_wide[:, part]
            gate = gate_wide[:, part]
            far = far_wide[:, part] * jnp.where(
                low, decay[:, 2 * p : 2 * p + 1], decay[:, 2 * p + 1 : 2 * p + 2]
            )
            fed = xs.astype(bf16)
            lows = jnp.where(low, fed, zero)
            highs = jnp.where(low, zero, fed)
            for (half, key, keys), score in zip(halves, masked):
                t = slice(half * LANES, (half + 1) * LANES)
                source = slice(key * LANES, (key + keys) * LANES)
                parts = []
                for h in (2 * p, 2 * p + 1):
                    differ = cum_col[t, h : h + 1] - cum_row[h : h + 1, source]
                    differ = jnp.minimum(differ, cap[h : h + 1, source])
                    parts.append(jnp.exp2(differ).astype(bf16) * score)
                y = jnp.dot(
                    jnp.concatenate(parts, axis=1),
                    jnp.concatenate([lows[source], highs[source]], axis=0),
                    preferred_element_type=f32,
                )
                v = (y + far[t] + tab[6:7, chans] * xs[t]) * gate[t]
                squares[half] = squares[half] + v * v
                out_rows = slice(s * BLOCK + half * LANES, s * BLOCK + (half + 1) * LANES)
                vg[out_rows, chans] = (v * tab[5:6, chans]).astype(bf16)
        summed = lax.dot_general(
            jnp.ones((8, LANES), f32),
            jnp.concatenate(squares, axis=0),
            NT,
            precision=highest,
            preferred_element_type=f32,
        )
        sq[:, rows] = summed[0:1]


def out_kernel(parity, vg, sq, w_own, a1, a2, a3, b1, b2, b3, out, g_all):
    first = iota((8, 2 * BLOCK), 0) == 0
    inverse = jnp.where(first, lax.rsqrt(sq[...] / 4096.0 + epsilon), 0.0)
    inverse = lax.dot_general(
        inverse, jnp.ones((8, LANES), f32), TN, precision=highest, preferred_element_type=f32
    )
    half = LANES
    for p in range(WIDE // half):
        chans = slice(p * half, (p + 1) * half)
        strands = [
            (vg[s * BLOCK : (s + 1) * BLOCK, chans].astype(f32) * inverse[s * BLOCK : (s + 1) * BLOCK])
            .astype(bf16)
            .astype(f32)
            for s in range(2)
        ]
        g = (strands[0] + strands[1]).astype(bf16)
        if p < 2:
            g_all[:, chans] = g
        else:
            at = (p - p % 2 + (parity[0] ^ (p % 2))) * half
            g_all[:, pl.ds(pl.multiple_of(at, half), half)] = g
    g = g_all[...]
    tile = 2 * LANES
    for n in range(out.shape[0] // 2):
        cols = slice(n * tile, (n + 1) * tile)
        weights = [w_own[:, cols]]
        for a, b in ((a1, b1), (a2, b2), (a3, b3)):
            weights.append(a[:, cols])
            weights.append(b[:, cols])
        result = jnp.dot(
            g, jnp.concatenate(weights, axis=0), preferred_element_type=f32
        ).astype(bf16)
        out[2 * n] = result[:, :LANES]
        out[2 * n + 1] = result[:, LANES:]


def build_tables(
    parity, w_out, embedding, norm_gain, w_z, w_x, w_bc, w_dt, dt_bias, a_log, d_skip, conv_x, conv_bc, gate_gain
):
    width = w_z.shape[1]
    given = (
        embedding,
        norm_gain[None],
        w_z,
        w_x,
        w_bc,
        w_dt.T,
        dt_bias[None],
        a_log[None],
        d_skip[None],
        conv_x,
        conv_bc,
        gate_gain[None],
    )
    return pl.pallas_call(
        table_kernel,
        in_specs=[pl.BlockSpec(memory_space=pltpu.SMEM)]
        + [pl.BlockSpec(memory_space=pltpu.HBM)] * (TABLE_ARGS + 1),
        out_specs=(
            pl.BlockSpec(memory_space=pltpu.VMEM),
            pl.BlockSpec(memory_space=pltpu.VMEM),
            pl.BlockSpec(memory_space=pltpu.VMEM),
        ),
        out_shape=(
            jax.ShapeDtypeStruct((32, width), f32),
            jax.ShapeDtypeStruct((32, w_bc.shape[1]), f32),
            jax.ShapeDtypeStruct((w_out.shape[0] // 2, w_out.shape[1]), w_out.dtype),
        ),
        scratch_shapes=[pltpu.VMEM((8, embedding.shape[1]), f32)]
        + [pltpu.VMEM(x.shape, x.dtype) for x in given]
        + [pltpu.SemaphoreType.DMA((TABLE_ARGS + 3 * (PIECES - 1),)), pltpu.SemaphoreType.DMA(())],
        compiler_params=pltpu.CompilerParams(vmem_limit_bytes=60 * 2**20),
        name="tables",
    )(parity, w_out, *given)


def prepare(place, complement, ids):
    smem = pl.BlockSpec(memory_space=pltpu.SMEM)
    vmem = pl.BlockSpec(memory_space=pltpu.VMEM)
    shape = jax.ShapeDtypeStruct
    return pl.pallas_call(
        prepare_kernel,
        in_specs=[smem, smem, vmem],
        out_specs=(vmem,) * 6,
        out_shape=(
            shape((ROWS, LANES), f32),
            shape((ROWS, LANES), f32),
            shape((TOKENS, ROWS, LANES), f32),
            shape((2 * BLOCK, LANES), bf16),
            shape((32, BLOCK), f32),
            shape((GRAMS, LANES), bf16),
        ),
        compiler_params=pltpu.CompilerParams(vmem_limit_bytes=32 * 2**20),
        name="prepare",
    )(place, complement, ids)


def run_block(place, prepared, tabs, cbc):
    smem = pl.BlockSpec(memory_space=pltpu.SMEM)
    vmem = pl.BlockSpec(memory_space=pltpu.VMEM)
    return pl.pallas_call(
        block_kernel,
        in_specs=[smem] + [vmem] * 11,
        out_specs=(vmem, vmem),
        out_shape=(
            jax.ShapeDtypeStruct((2 * BLOCK, WIDE), bf16),
            jax.ShapeDtypeStruct((1, 2 * BLOCK), f32),
        ),
        compiler_params=pltpu.CompilerParams(vmem_limit_bytes=48 * 2**20),
        cost_estimate=pl.CostEstimate(
            flops=40 * 10**9, bytes_accessed=100 * 2**20, transcendentals=10**7
        ),
        name="block",
    )(place, *prepared, *tabs, cbc)


def run_out(parity, vg, sq, w_own, mine, theirs):
    features = w_own.shape[1]
    smem = pl.BlockSpec(memory_space=pltpu.SMEM)
    vmem = pl.BlockSpec(memory_space=pltpu.VMEM)
    return pl.pallas_call(
        out_kernel,
        in_specs=[smem] + [vmem] * 9,
        out_specs=vmem,
        out_shape=jax.ShapeDtypeStruct((features // LANES, BLOCK, LANES), bf16),
        scratch_shapes=[pltpu.VMEM((BLOCK, WIDE), bf16)],
        compiler_params=pltpu.CompilerParams(vmem_limit_bytes=40 * 2**20),
        name="project",
    )(parity, vg, sq, w_own, *mine, *theirs)


def swap(x, axis, distance):
    count = lax.axis_size(axis)
    return lax.ppermute(x, axis, [(i, i ^ distance) for i in range(count)])


def local(
    ids,
    complement,
    embedding,
    norm_gain,
    w_z,
    w_x,
    w_bc,
    w_dt,
    dt_bias,
    a_log,
    conv_x,
    conv_bc,
    d_skip,
    gate_gain,
    w_out,
):
    context = lax.axis_index("context").astype(i32)
    tensor = lax.axis_index("tensor").astype(i32)
    parity = context % 2
    count = lax.axis_size("context")
    spread = jnp.broadcast_to(ids.reshape(1, -1, LANES), (count, ids.shape[0] // LANES, LANES))
    everyone = lax.all_to_all(spread, "context", 0, 0, tiled=True).reshape(ROWS, LANES)
    place = (context * (ids.shape[0] // LANES) + (tensor % 4) * (BLOCK // LANES)).reshape(1)
    tab, cbc, share = build_tables(
        parity.reshape(1), w_out, embedding, norm_gain, w_z, w_x, w_bc, w_dt, dt_bias, a_log, d_skip, conv_x, conv_bc, gate_gain
    )
    tab, everyone, share = lax.optimization_barrier((tab, everyone, share))
    tabs = [tab] + [swap(tab, "tensor", d) for d in (1, 2, 3)]
    everyone, tabs[1] = lax.optimization_barrier((everyone, tabs[1]))
    prepared = prepare(place, complement, everyone)
    mine = [swap(share, "tensor", d) for d in (1, 2, 3)]

    vg, sq = run_block(place, prepared, tabs, cbc)
    sq = lax.psum(sq, "tensor", axis_index_groups=SAME_POSITIONS)
    sq, *mine = lax.optimization_barrier((sq, *mine))
    theirs = [swap(x, "context", 1) for x in mine]
    terms = run_out(parity.reshape(1), vg, sq, w_out, mine, theirs)
    arrived = lax.all_to_all(terms, "tensor", 0, 0, tiled=True)
    summed = jnp.sum(arrived.astype(f32).reshape(4, 4, BLOCK, LANES), axis=0)
    return summed.reshape(4 * BLOCK, LANES).astype(bf16)


def solution(mesh):
    placed = (
        P("context"),
        P(),
        P(),
        P(),
        P(None, "tensor"),
        P(None, "tensor"),
        P(),
        P(None, "tensor"),
        P("tensor"),
        P("tensor"),
        P(None, "tensor"),
        P(),
        P("tensor"),
        P("tensor"),
        P("tensor", None),
    )
    return jax.shard_map(
        local, mesh=mesh, in_specs=placed, out_specs=P("context", "tensor"), check_vma=False
    )
```

```python
import functools

import jax
import jax.numpy as jnp
from jax import lax
from jax.experimental import pallas as pl
from jax.experimental.pallas import tpu as pltpu
from jax.sharding import PartitionSpec as P

f32 = jnp.float32
bf16 = jnp.bfloat16
i32 = jnp.int32
highest = lax.Precision.HIGHEST
epsilon = 1e-05

LANES = 128
SEQ = 16384
ROWS = SEQ // LANES
BLOCK = 256
STATE = 128
HEAD = 64
TOKENS = 5
NONE = 5
LOG2E = 1.4426950408889634
TINY = 2.0**-126
WIDE = 1024
HEADS = WIDE // HEAD
GRAMS = 144
TABLE_ARGS = 12
PIECES = 4

QUARTERS = [[t for t in range(16) if (t // 2 + 2 * (t % 2) + 3) % 4 == q] for q in range(4)]
PEERS = (
    [(t, (t + 2) % 16) for t in range(16)],
    [(t, (t - 2) % 16) for t in range(16)],
    [(t, t ^ 1) for t in range(16)],
)

TN = (((0,), (0,)), ((), ()))
NT = (((1,), (1,)), ((), ()))


def iota(shape, dim):
    return lax.broadcasted_iota(i32, shape, dim)


def silu(v):
    half = 0.5 * v
    return half + half * jnp.tanh(half)


def split(x, terms=3):
    parts = []
    for _ in range(terms):
        part = x.astype(bf16)
        parts.append(part)
        x = x - part.astype(f32)
    return parts


def table_kernel(parity, w_out, *refs):
    given = refs[:TABLE_ARGS]
    tab, cbc, share, rows = refs[TABLE_ARGS : TABLE_ARGS + 4]
    held = refs[TABLE_ARGS + 4 : -2]
    arrived, shared = refs[-2:]
    half = share.shape[0]
    part = w_out.at[pl.ds(pl.multiple_of(parity[0] * half, half), half), :]
    copies = []
    for source, target in zip(given, held):
        count = PIECES if source.shape[0] > 1024 else 1
        size = source.shape[0] // count
        for n in range(count):
            span = pl.ds(n * size, size)
            one = (source, target) if count == 1 else (source.at[span, :], target.at[span, :])
            copies.append(pltpu.make_async_copy(*one, arrived.at[len(copies)]))
    for copy in copies:
        copy.start()
    kept = pltpu.make_async_copy(part, share, shared)
    kept.start()
    for copy in copies:
        copy.wait()
    emb, gain, wz, wx, wbc, wdt, bias, alog, dskip, convx, convbc, ggain = held
    rows[...] = jnp.zeros_like(rows)
    rows[0:TOKENS, :] = emb[...].astype(f32)
    e = rows[...]
    normed = (
        e * lax.rsqrt(jnp.mean(e * e, axis=-1, keepdims=True) + epsilon) * gain[...]
    ).astype(bf16)

    def project(w):
        return jnp.dot(normed, w[...], preferred_element_type=f32)

    z = project(wz).astype(bf16).astype(f32)
    xs = project(wx).astype(bf16).astype(f32)
    bc = project(wbc).astype(bf16).astype(f32)
    raw = lax.dot_general(normed, wdt[...], NT, preferred_element_type=f32) + bias[...]
    dt = jnp.maximum(raw, 0.0) + jnp.log1p(jnp.exp(-jnp.abs(raw)))
    width = z.shape[1]

    def spread(v):
        lane = iota((v.shape[0], width), 1)
        out = jnp.broadcast_to(v[:, 0:1], lane.shape)
        for h in range(1, v.shape[1]):
            out = jnp.where(lane >= h * HEAD, v[:, h : h + 1], out)
        return out

    row = iota((8, width), 0)
    own = jnp.where(row == 6, spread(dskip[...]), spread(jnp.exp(alog[...])))
    own = jnp.where(row == 5, ggain[...], own)
    tab[0:8, :] = jnp.where(row < TOKENS, silu(z), own)
    tab[8:16, :] = xs
    tab[16:24, :] = jnp.zeros((8, width), f32)
    tab[16:20, :] = convx[...]
    tab[24:32, :] = jnp.where(row < TOKENS, spread(dt), 0.0)
    for k in range(4):
        cbc[8 * k : 8 * k + 8, :] = convbc[k : k + 1, :] * bc
    kept.wait()


def prepare_kernel(
    place, comp, ids_ref, grams, side_tok, count, hot_taps, own_rows, older
):
    r0 = place[0]
    ids = ids_ref[...]
    row = iota((ROWS, LANES), 0)
    lane = iota((ROWS, LANES), 1)
    at = row * LANES + lane
    flip = jnp.zeros_like(ids)
    for k in range(TOKENS):
        flip = jnp.where(ids == k, comp[k], flip)

    def before(x):
        y = pltpu.roll(x, 1, 1)
        y = jnp.where(lane == 0, pltpu.roll(y, 1, 0), y)
        return jnp.where(at == 0, NONE, y)

    def after(x):
        y = pltpu.roll(x, LANES - 1, 1)
        y = jnp.where(lane == LANES - 1, pltpu.roll(y, ROWS - 1, 0), y)
        return jnp.where(at == SEQ - 1, NONE, y)

    fs = [ids]
    rs = [flip]
    for k in range(3):
        fs.append(before(fs[-1]))
        rs.append(after(rs[-1]))
    g_f = 25 * fs[3] + 5 * fs[2] + fs[1]
    g_r = 25 * rs[3] + 5 * rs[2] + rs[1]
    for k in range(3):
        g_f = jnp.where(at == k, 125 + k, g_f)
        g_r = jnp.where(at == SEQ - 1 - k, 125 if k == 0 else 127 + k, g_r)
    ahead = row < r0
    tok = jnp.where(ahead, ids, flip)
    tok = jnp.where(ahead | (row > r0 + 1), tok, -1)
    grams[...] = jnp.where(ahead, g_f, g_r).astype(f32)
    side_tok[...] = tok.astype(f32)

    hot = [jnp.where(tok == k, 1.0, 0.0) for k in range(TOKENS)]
    hots = jnp.concatenate(hot, axis=0).astype(bf16)
    strict = jnp.where(row < lane, 1.0, 0.0).astype(bf16)
    prior = jnp.dot(hots, strict, preferred_element_type=f32)
    total = jnp.dot(hots, jnp.ones((LANES, LANES), bf16), preferred_element_type=f32)
    between = ((row < lane) & (lane < r0)) | ((lane > r0 + 1) & (lane < row))
    between = jnp.where(between, 1.0, 0.0).astype(bf16)
    for k in range(TOKENS):
        part = slice(k * ROWS, (k + 1) * ROWS)
        far = jnp.dot(between, total[part].astype(bf16), preferred_element_type=f32)
        near = jnp.where(ahead, total[part] - prior[part] - hot[k], prior[part])
        count[k] = near + far

    g = iota((GRAMS, LANES), 0)
    col = iota((GRAMS, LANES), 1)
    d0 = sum(jnp.where(g >= 25 * m, 1, 0) for m in range(1, TOKENS))
    rest = g - 25 * d0
    d1 = sum(jnp.where(rest >= 5 * m, 1, 0) for m in range(1, TOKENS))
    d2 = rest - 5 * d1
    plain = g < 125
    d0 = jnp.where(plain, d0, NONE)
    d1 = jnp.where(plain, d1, NONE)
    d2 = jnp.where(plain, d2, NONE)
    d1 = jnp.where(g == 127, ids[0:1, 0:1], d1)
    d2 = jnp.where(g == 126, ids[0:1, 0:1], d2)
    d2 = jnp.where(g == 127, ids[0:1, 1:2], d2)
    d1 = jnp.where(g == 129, flip[ROWS - 1 :, LANES - 1 :], d1)
    d2 = jnp.where(g == 128, flip[ROWS - 1 :, LANES - 1 :], d2)
    d2 = jnp.where(g == 129, flip[ROWS - 1 :, LANES - 2 : LANES - 1], d2)
    tap = (col >> 3) % 3
    digit = jnp.where(tap == 0, d0, jnp.where(tap == 1, d1, d2))
    older[...] = jnp.where((digit == (col & 7)) & (col < 72), 1.0, 0.0).astype(bf16)

    place_row = iota((32, BLOCK), 0)
    lane_b = iota((BLOCK, BLOCK), 1)
    row_b = iota((BLOCK, BLOCK), 0)

    def own(x):
        first = jnp.sum(jnp.where(row == r0, x, 0), axis=0, keepdims=True)
        second = jnp.sum(jnp.where(row == r0 + 1, x, 0), axis=0, keepdims=True)
        return jnp.concatenate([first, second], axis=1)

    for s, values in enumerate((fs, rs)):
        digit = own(values[0])
        for k in range(3):
            digit = jnp.where(place_row < 8 * (3 - k), own(values[k + 1]), digit)
        hot_own = jnp.where(digit == (place_row & 7), 1.0, 0.0)
        now = hot_own[24:32]
        inclusive = (row_b <= lane_b) if s == 0 else (row_b >= lane_b)
        inclusive = jnp.where(inclusive, 1.0, 0.0).astype(bf16)
        counts = jnp.dot(now.astype(bf16), inclusive, preferred_element_type=f32)
        own_rows[16 * s : 16 * s + 8, :] = counts
        own_rows[16 * s + 8 : 16 * s + 16, :] = now
        hot_taps[s * BLOCK : (s + 1) * BLOCK, :] = jnp.concatenate(
            [hot_own] * 2 + [now] * 2 + [counts] * 3 + [jnp.zeros((24, BLOCK), f32)], axis=0
        ).T.astype(bf16)


def block_kernel(
    place, grams, side_tok, count, hot_taps, own_rows, older, t0, t1, t2, t3, cbc, vg, sq
):
    chunk = place[0] // 8
    r0 = place[0]
    tab = jnp.concatenate([t0[...], t1[...], t2[...], t3[...]], axis=1)
    dt_tab = tab[24:32]
    rate_tab = tab[7:8] * dt_tab * LOG2E
    log_tab = jnp.log2(jnp.maximum(dt_tab, TINY))
    pick = jnp.where(iota((HEADS, WIDE), 1) == HEAD * iota((HEADS, WIDE), 0), 1.0, 0.0).astype(bf16)

    def stack(*parts):
        return jnp.concatenate([part.astype(f32) for part in parts], axis=0).astype(bf16)

    spare = jnp.zeros((8, WIDE), f32)
    both_tab = stack(*split(rate_tab), *split(log_tab), spare, spare)
    both = lax.dot_general(pick, both_tab, NT, preferred_element_type=f32)
    rate = both[:, 0:8] + both[:, 8:16] + both[:, 16:24]
    log_dt = both[:, 24:32] + both[:, 32:40] + both[:, 40:48]
    both_t = lax.dot_general(both_tab, pick, NT, preferred_element_type=f32)
    rate_t = both_t[0:8] + both_t[8:16] + both_t[16:24]
    columns = [jnp.broadcast_to(-rate[:, k : k + 1], (HEADS, BLOCK)) for k in range(TOKENS)]

    def pair(ref, r):
        return jnp.concatenate([ref[pl.ds(r, 1), :], ref[pl.ds(r + 1, 1), :]], axis=1)

    nothing = jnp.zeros((HEADS, BLOCK), bf16)

    def weigh(r):
        token = jnp.broadcast_to(pair(side_tok, r), (HEADS, BLOCK)).astype(bf16)
        exponent = columns[0] * pair(count.at[0], r)
        for k in range(1, TOKENS):
            exponent = exponent + columns[k] * pair(count.at[k], r)
        weight = jnp.exp2(exponent)
        return token, weight

    def by_token(token, weight):
        return [jnp.where(token == k, weight, nothing) for k in range(TOKENS)]

    gram_row = iota((GRAMS, BLOCK), 0).astype(bf16)
    one = jnp.ones((GRAMS, BLOCK), bf16)
    none = jnp.zeros((GRAMS, BLOCK), bf16)

    def window(r):
        kind = jnp.broadcast_to(pair(grams, r), (GRAMS, BLOCK)).astype(bf16)
        return jnp.where(gram_row == kind, one, none)

    def tally(seen, weights):
        return lax.dot_general(
            jnp.concatenate(seen, axis=1),
            jnp.concatenate(weights, axis=1),
            NT,
            preferred_element_type=f32,
        )

    sides = [jnp.zeros((GRAMS, TOKENS * HEADS), f32) for _ in range(2)]
    for step in range(ROWS // 8):
        weights = []
        for j in range(4):
            token, weight = weigh(8 * step + 2 * j)
            weights.append(jnp.concatenate(by_token(token, weight.astype(bf16)), axis=0))
        part = tally([window(8 * step + 2 * j) for j in range(4)], weights)
        sides[0] = sides[0] + part * jnp.where(step < chunk, 1.0, 0.0)
        sides[1] = sides[1] + part * jnp.where(step > chunk, 1.0, 0.0)
    weights = []
    for j in range(4):
        r = pl.multiple_of(8 * chunk, 8) + 2 * j
        token, weight = weigh(r)
        first = jnp.where(r < r0, 1.0, 0.0)
        forward = by_token(token, (weight * first).astype(bf16))
        reverse = by_token(token, (weight * (1.0 - first)).astype(bf16))
        weights.append(jnp.concatenate(forward + reverse, axis=0))
    part = tally([window(pl.multiple_of(8 * chunk, 8) + 2 * j) for j in range(4)], weights)
    hist = (part + jnp.concatenate(sides, axis=1)).astype(bf16)

    taps = jnp.concatenate([tab[16 + k : 17 + k] * tab[8:16] for k in range(4)], axis=0)
    bc_taps = cbc[...]
    kinds = older[...]
    rest = jnp.zeros((56, WIDE), f32)
    x_older = jnp.dot(kinds, stack(*split(taps[0:24]), rest), preferred_element_type=f32)
    b_older = jnp.dot(
        kinds, stack(*split(bc_taps[0:24, :STATE]), rest[:, :STATE]), preferred_element_type=f32
    )
    lift = iota((HEADS, WIDE), 1) - HEAD * iota((HEADS, WIDE), 0)
    lift = jnp.where((lift >= 0) & (lift < HEAD), 1.0, 0.0).astype(bf16)
    feeds = []
    moved = [[], []]
    for k in range(TOKENS):
        feeds.append(silu(b_older + bc_taps[24 + k : 25 + k, :STATE]).astype(bf16))
        act = (silu(x_older + taps[24 + k : 25 + k]) * dt_tab[k : k + 1]).astype(bf16)
        for s in range(2):
            start = (s * TOKENS + k) * HEADS
            part = jnp.dot(hist[:, start : start + HEADS], lift, preferred_element_type=f32)
            moved[s].append(act * part.astype(bf16))
    feeds = jnp.concatenate(feeds, axis=0)
    entering = [
        lax.dot_general(
            feeds, jnp.concatenate(moved[s], axis=0), TN, preferred_element_type=f32
        ).astype(bf16)
        for s in range(2)
    ]

    def look(hots, table):
        return jnp.dot(hots, table, preferred_element_type=f32)

    def blank(count, width):
        return jnp.zeros((count, width), f32)

    gate_tab = jnp.where(iota((8, WIDE), 0) < TOKENS, tab[0:8], 0.0)
    taps2 = stack(*split(taps, 2), blank(64, WIDE))
    bc2 = stack(*split(bc_taps, 2), blank(64, 2 * STATE))
    gate2 = stack(blank(64, WIDE), *split(gate_tab, 2), blank(48, WIDE))
    rate3 = stack(blank(80, HEADS), *split(rate_t), blank(24, HEADS))
    cap = jnp.broadcast_to(jnp.max(log_dt[:, :TOKENS], axis=1, keepdims=True), (HEADS, BLOCK))
    row_tab = jnp.concatenate([rate, log_dt], axis=1)
    lane_h = iota((LANES, LANES), 1)
    row_h = iota((LANES, LANES), 0)
    low = iota((BLOCK, LANES), 1) < HEAD
    zero = jnp.zeros((BLOCK, LANES), bf16)
    for s in range(2):
        rows = slice(s * BLOCK, (s + 1) * BLOCK)
        hot = hot_taps[rows, :]
        bc_act = silu(look(hot, bc2))
        feed = bc_act[:, :STATE].astype(bf16)
        read = bc_act[:, STATE:].astype(bf16)
        scores = lax.dot_general(read, feed, NT, preferred_element_type=f32)
        cum_row = -jnp.dot(
            row_tab, own_rows[16 * s : 16 * s + 16, :], precision=highest, preferred_element_type=f32
        )
        cum_col = -look(hot, rate3)
        decay = jnp.exp2(cum_col)
        near = (lane_h <= row_h) if s == 0 else (lane_h >= row_h)
        halves = ((0, 0, 1), (1, 0, 2)) if s == 0 else ((0, 0, 2), (1, 1, 1))
        masked = []
        for half, key, keys in halves:
            t = slice(half * LANES, (half + 1) * LANES)
            pieces = []
            for j in range(key, key + keys):
                piece = scores[t, j * LANES : (j + 1) * LANES]
                pieces.append(jnp.where(near, piece, 0.0) if j == half else piece)
            masked.append(jnp.concatenate(pieces, axis=1).astype(bf16))
        squares = [jnp.zeros((LANES, LANES), f32) for _ in range(2)]
        for p in range(HEADS // 2):
            chans = slice(p * LANES, (p + 1) * LANES)
            if p % 2 == 0:
                wide = slice(p * LANES, (p + 2) * LANES)
                xs_wide = silu(look(hot, taps2[:, wide]))
                gate_wide = look(hot, gate2[:, wide])
                far_wide = look(read, entering[s][:, wide])
            part = slice((p % 2) * LANES, (p % 2 + 1) * LANES)
            xs = xs_wide[:, part]
            gate = gate_wide[:, part]
            far = far_wide[:, part] * jnp.where(
                low, decay[:, 2 * p : 2 * p + 1], decay[:, 2 * p + 1 : 2 * p + 2]
            )
            fed = xs.astype(bf16)
            lows = jnp.where(low, fed, zero)
            highs = jnp.where(low, zero, fed)
            for (half, key, keys), score in zip(halves, masked):
                t = slice(half * LANES, (half + 1) * LANES)
                source = slice(key * LANES, (key + keys) * LANES)
                parts = []
                for h in (2 * p, 2 * p + 1):
                    differ = cum_col[t, h : h + 1] - cum_row[h : h + 1, source]
                    differ = jnp.minimum(differ, cap[h : h + 1, source])
                    parts.append(jnp.exp2(differ).astype(bf16) * score)
                y = jnp.dot(
                    jnp.concatenate(parts, axis=1),
                    jnp.concatenate([lows[source], highs[source]], axis=0),
                    preferred_element_type=f32,
                )
                v = (y + far[t] + tab[6:7, chans] * xs[t]) * gate[t]
                squares[half] = squares[half] + v * v
                out_rows = slice(s * BLOCK + half * LANES, s * BLOCK + (half + 1) * LANES)
                vg[out_rows, chans] = (v * tab[5:6, chans]).astype(bf16)
        summed = lax.dot_general(
            jnp.ones((8, LANES), f32),
            jnp.concatenate(squares, axis=0),
            NT,
            precision=highest,
            preferred_element_type=f32,
        )
        sq[:, rows] = summed[0:1]


def out_kernel(parity, vg, sq, w_own, a1, a2, a3, b1, b2, b3, out, g_all):
    first = iota((8, 2 * BLOCK), 0) == 0
    inverse = jnp.where(first, lax.rsqrt(sq[...] / 4096.0 + epsilon), 0.0)
    inverse = lax.dot_general(
        inverse, jnp.ones((8, LANES), f32), TN, precision=highest, preferred_element_type=f32
    )
    half = LANES
    for p in range(WIDE // half):
        chans = slice(p * half, (p + 1) * half)
        strands = [
            (vg[s * BLOCK : (s + 1) * BLOCK, chans].astype(f32) * inverse[s * BLOCK : (s + 1) * BLOCK])
            .astype(bf16)
            .astype(f32)
            for s in range(2)
        ]
        g = (strands[0] + strands[1]).astype(bf16)
        if p < 2:
            g_all[:, chans] = g
        else:
            at = (p - p % 2 + (parity[0] ^ (p % 2))) * half
            g_all[:, pl.ds(pl.multiple_of(at, half), half)] = g
    g = g_all[...]
    tile = 2 * LANES
    for n in range(out.shape[0] // 2):
        cols = slice(n * tile, (n + 1) * tile)
        weights = [w_own[:, cols]]
        for a, b in ((a1, b1), (a2, b2), (a3, b3)):
            weights.append(a[:, cols])
            weights.append(b[:, cols])
        result = jnp.dot(
            g, jnp.concatenate(weights, axis=0), preferred_element_type=f32
        ).astype(bf16)
        out[2 * n] = result[:, :LANES]
        out[2 * n + 1] = result[:, LANES:]


def build_tables(
    parity, w_out, embedding, norm_gain, w_z, w_x, w_bc, w_dt, dt_bias, a_log, d_skip, conv_x, conv_bc, gate_gain
):
    width = w_z.shape[1]
    given = (
        embedding,
        norm_gain[None],
        w_z,
        w_x,
        w_bc,
        w_dt.T,
        dt_bias[None],
        a_log[None],
        d_skip[None],
        conv_x,
        conv_bc,
        gate_gain[None],
    )
    return pl.pallas_call(
        table_kernel,
        in_specs=[pl.BlockSpec(memory_space=pltpu.SMEM)]
        + [pl.BlockSpec(memory_space=pltpu.HBM)] * (TABLE_ARGS + 1),
        out_specs=(
            pl.BlockSpec(memory_space=pltpu.VMEM),
            pl.BlockSpec(memory_space=pltpu.VMEM),
            pl.BlockSpec(memory_space=pltpu.VMEM),
        ),
        out_shape=(
            jax.ShapeDtypeStruct((32, width), f32),
            jax.ShapeDtypeStruct((32, w_bc.shape[1]), f32),
            jax.ShapeDtypeStruct((w_out.shape[0] // 2, w_out.shape[1]), w_out.dtype),
        ),
        scratch_shapes=[pltpu.VMEM((8, embedding.shape[1]), f32)]
        + [pltpu.VMEM(x.shape, x.dtype) for x in given]
        + [pltpu.SemaphoreType.DMA((TABLE_ARGS + 3 * (PIECES - 1),)), pltpu.SemaphoreType.DMA(())],
        compiler_params=pltpu.CompilerParams(vmem_limit_bytes=60 * 2**20),
        name="tables",
    )(parity, w_out, *given)


def prepare(place, complement, ids):
    smem = pl.BlockSpec(memory_space=pltpu.SMEM)
    vmem = pl.BlockSpec(memory_space=pltpu.VMEM)
    shape = jax.ShapeDtypeStruct
    return pl.pallas_call(
        prepare_kernel,
        in_specs=[smem, smem, vmem],
        out_specs=(vmem,) * 6,
        out_shape=(
            shape((ROWS, LANES), f32),
            shape((ROWS, LANES), f32),
            shape((TOKENS, ROWS, LANES), f32),
            shape((2 * BLOCK, LANES), bf16),
            shape((32, BLOCK), f32),
            shape((GRAMS, LANES), bf16),
        ),
        compiler_params=pltpu.CompilerParams(vmem_limit_bytes=32 * 2**20),
        name="prepare",
    )(place, complement, ids)


def run_block(place, prepared, tabs, cbc):
    smem = pl.BlockSpec(memory_space=pltpu.SMEM)
    vmem = pl.BlockSpec(memory_space=pltpu.VMEM)
    return pl.pallas_call(
        block_kernel,
        in_specs=[smem] + [vmem] * 11,
        out_specs=(vmem, vmem),
        out_shape=(
            jax.ShapeDtypeStruct((2 * BLOCK, WIDE), bf16),
            jax.ShapeDtypeStruct((1, 2 * BLOCK), f32),
        ),
        compiler_params=pltpu.CompilerParams(vmem_limit_bytes=48 * 2**20),
        cost_estimate=pl.CostEstimate(
            flops=40 * 10**9, bytes_accessed=100 * 2**20, transcendentals=10**7
        ),
        name="block",
    )(place, *prepared, *tabs, cbc)


def run_out(parity, vg, sq, w_own, mine, theirs):
    features = w_own.shape[1]
    smem = pl.BlockSpec(memory_space=pltpu.SMEM)
    vmem = pl.BlockSpec(memory_space=pltpu.VMEM)
    return pl.pallas_call(
        out_kernel,
        in_specs=[smem] + [vmem] * 9,
        out_specs=vmem,
        out_shape=jax.ShapeDtypeStruct((features // LANES, BLOCK, LANES), bf16),
        scratch_shapes=[pltpu.VMEM((BLOCK, WIDE), bf16)],
        compiler_params=pltpu.CompilerParams(vmem_limit_bytes=40 * 2**20),
        name="project",
    )(parity, vg, sq, w_own, *mine, *theirs)


def from_peers(x):
    return [lax.ppermute(x, "tensor", pairs) for pairs in PEERS]


def other_core(x):
    count = lax.axis_size("context")
    return lax.ppermute(x, "context", [(i, i ^ 1) for i in range(count)])


def local(
    ids,
    complement,
    embedding,
    norm_gain,
    w_z,
    w_x,
    w_bc,
    w_dt,
    dt_bias,
    a_log,
    conv_x,
    conv_bc,
    d_skip,
    gate_gain,
    w_out,
):
    context = lax.axis_index("context").astype(i32)
    tensor = lax.axis_index("tensor").astype(i32)
    parity = context % 2
    count = lax.axis_size("context")
    spread = jnp.broadcast_to(ids.reshape(1, -1, LANES), (count, ids.shape[0] // LANES, LANES))
    everyone = lax.all_to_all(spread, "context", 0, 0, tiled=True).reshape(ROWS, LANES)
    quarter = (tensor // 2 + 2 * (tensor % 2) + 3) % 4
    place = (context * (ids.shape[0] // LANES) + quarter * (BLOCK // LANES)).reshape(1)
    tab, cbc, share = build_tables(
        parity.reshape(1), w_out, embedding, norm_gain, w_z, w_x, w_bc, w_dt, dt_bias, a_log, d_skip, conv_x, conv_bc, gate_gain
    )
    tab, everyone, share = lax.optimization_barrier((tab, everyone, share))
    tabs = [tab] + from_peers(tab)
    everyone, tabs[1] = lax.optimization_barrier((everyone, tabs[1]))
    prepared = prepare(place, complement, everyone)
    mine = from_peers(share)

    vg, sq = run_block(place, prepared, tabs, cbc)
    vg, sq, *mine = lax.optimization_barrier((vg, sq, *mine))
    theirs = [other_core(x) for x in mine]
    sq = lax.psum(sq, "tensor", axis_index_groups=QUARTERS)
    terms = run_out(parity.reshape(1), vg, sq, w_out, mine, theirs)
    arrived = lax.all_to_all(terms, "tensor", 0, 0, tiled=True)
    summed = [sum(arrived[t].astype(f32) for t in members) for members in QUARTERS]
    return jnp.concatenate(summed, axis=0).astype(bf16)


def solution(mesh):
    placed = (
        P("context"),
        P(),
        P(),
        P(),
        P(None, "tensor"),
        P(None, "tensor"),
        P(),
        P(None, "tensor"),
        P("tensor"),
        P("tensor"),
        P(None, "tensor"),
        P(),
        P("tensor"),
        P("tensor"),
        P("tensor", None),
    )
    return jax.shard_map(
        local, mesh=mesh, in_specs=placed, out_specs=P("context", "tensor"), check_vma=False
    )
```

```python
import functools

import jax
import jax.numpy as jnp
from jax import lax
from jax.experimental import pallas as pl
from jax.experimental.pallas import tpu as pltpu
from jax.sharding import PartitionSpec as P

f32 = jnp.float32
bf16 = jnp.bfloat16
i32 = jnp.int32
highest = lax.Precision.HIGHEST
epsilon = 1e-05

LANES = 128
SEQ = 16384
ROWS = SEQ // LANES
BLOCK = 256
STATE = 128
HEAD = 64
TOKENS = 5
NONE = 5
LOG2E = 1.4426950408889634
TINY = 2.0**-126
WIDE = 1024
HEADS = WIDE // HEAD
GRAMS = 144
TABLE_ARGS = 12
PIECES = 4

QUARTERS = [[t for t in range(16) if (t // 2 + 2 * (t % 2) + 3) % 4 == q] for q in range(4)]
PEERS = (
    [(t, (t + 2) % 16) for t in range(16)],
    [(t, (t - 2) % 16) for t in range(16)],
    [(t, t ^ 1) for t in range(16)],
)

TN = (((0,), (0,)), ((), ()))
NT = (((1,), (1,)), ((), ()))


def iota(shape, dim):
    return lax.broadcasted_iota(i32, shape, dim)


def silu(v):
    half = 0.5 * v
    return half + half * jnp.tanh(half)


def split(x, terms=3):
    parts = []
    for _ in range(terms):
        part = x.astype(bf16)
        parts.append(part)
        x = x - part.astype(f32)
    return parts


def table_kernel(parity, ids, w_out, *refs):
    given = refs[:TABLE_ARGS]
    tab, share, spread, rows = refs[TABLE_ARGS : TABLE_ARGS + 4]
    held = refs[TABLE_ARGS + 4 : -2]
    arrived, shared = refs[-2:]
    half = share.shape[0]
    part = w_out.at[pl.ds(pl.multiple_of(parity[0] * half, half), half), :]
    groups = []
    used = 0
    for source, target in zip(given, held):
        count = PIECES if source.shape[0] > 1024 else 1
        size = source.shape[0] // count
        group = []
        for n in range(count):
            span = pl.ds(n * size, size)
            one = (source, target) if count == 1 else (source.at[span, :], target.at[span, :])
            group.append(pltpu.make_async_copy(*one, arrived.at[used]))
            used += 1
        groups.append(group)
    for group in sorted(groups, key=len):
        for copy in group:
            copy.start()
    kept = pltpu.make_async_copy(part, share, shared)
    kept.start()
    spread[...] = jnp.broadcast_to(ids[...][None], spread.shape)
    for group in groups:
        if len(group) == 1:
            group[0].wait()
    emb, gain, wz, wx, wbc, wdt, bias, alog, dskip, convx, convbc, ggain = held
    rows[...] = jnp.zeros_like(rows)
    rows[0:TOKENS, :] = emb[...].astype(f32)
    e = rows[...]
    normed = (
        e * lax.rsqrt(jnp.mean(e * e, axis=-1, keepdims=True) + epsilon) * gain[...]
    ).astype(bf16)

    def project(w, group):
        for copy in group:
            copy.wait()
        return jnp.dot(normed, w[...], preferred_element_type=f32)

    z = project(wz, groups[2]).astype(bf16).astype(f32)
    xs = project(wx, groups[3]).astype(bf16).astype(f32)
    bc = project(wbc, groups[4]).astype(bf16).astype(f32)
    raw = lax.dot_general(normed, wdt[...], NT, preferred_element_type=f32) + bias[...]
    dt = jnp.maximum(raw, 0.0) + jnp.log1p(jnp.exp(-jnp.abs(raw)))
    width = z.shape[1]

    def spread(v):
        lane = iota((v.shape[0], width), 1)
        out = jnp.broadcast_to(v[:, 0:1], lane.shape)
        for h in range(1, v.shape[1]):
            out = jnp.where(lane >= h * HEAD, v[:, h : h + 1], out)
        return out

    row = iota((8, width), 0)
    own = jnp.where(row == 6, spread(dskip[...]), spread(jnp.exp(alog[...])))
    own = jnp.where(row == 5, ggain[...], own)
    tab[0:8, :] = jnp.where(row < TOKENS, silu(z), own)
    tab[8:16, :] = xs
    tab[16:24, :] = jnp.zeros((8, width), f32)
    tab[16:20, :] = convx[...]
    tab[24:32, :] = jnp.where(row < TOKENS, spread(dt), 0.0)
    for k in range(4):
        tab[32 + 8 * k : 40 + 8 * k, :] = convbc[k : k + 1, :] * bc
    kept.wait()


def prepare_kernel(
    place, comp, ids_ref, grams, side_tok, count, hot_taps, own_rows, older
):
    r0 = place[0]
    ids = ids_ref[...]
    row = iota((ROWS, LANES), 0)
    lane = iota((ROWS, LANES), 1)
    at = row * LANES + lane
    flip = jnp.zeros_like(ids)
    for k in range(TOKENS):
        flip = jnp.where(ids == k, comp[k], flip)

    def before(x):
        y = pltpu.roll(x, 1, 1)
        y = jnp.where(lane == 0, pltpu.roll(y, 1, 0), y)
        return jnp.where(at == 0, NONE, y)

    def after(x):
        y = pltpu.roll(x, LANES - 1, 1)
        y = jnp.where(lane == LANES - 1, pltpu.roll(y, ROWS - 1, 0), y)
        return jnp.where(at == SEQ - 1, NONE, y)

    fs = [ids]
    rs = [flip]
    for k in range(3):
        fs.append(before(fs[-1]))
        rs.append(after(rs[-1]))
    g_f = 25 * fs[3] + 5 * fs[2] + fs[1]
    g_r = 25 * rs[3] + 5 * rs[2] + rs[1]
    for k in range(3):
        g_f = jnp.where(at == k, 125 + k, g_f)
        g_r = jnp.where(at == SEQ - 1 - k, 125 if k == 0 else 127 + k, g_r)
    ahead = row < r0
    tok = jnp.where(ahead, ids, flip)
    tok = jnp.where(ahead | (row > r0 + 1), tok, -1)
    grams[...] = jnp.where(ahead, g_f, g_r).astype(f32)
    side_tok[...] = tok.astype(f32)

    hot = [jnp.where(tok == k, 1.0, 0.0) for k in range(TOKENS)]
    hots = jnp.concatenate(hot, axis=0).astype(bf16)
    strict = jnp.where(row < lane, 1.0, 0.0).astype(bf16)
    prior = jnp.dot(hots, strict, preferred_element_type=f32)
    total = jnp.dot(hots, jnp.ones((LANES, LANES), bf16), preferred_element_type=f32)
    between = ((row < lane) & (lane < r0)) | ((lane > r0 + 1) & (lane < row))
    between = jnp.where(between, 1.0, 0.0).astype(bf16)
    for k in range(TOKENS):
        part = slice(k * ROWS, (k + 1) * ROWS)
        far = jnp.dot(between, total[part].astype(bf16), preferred_element_type=f32)
        near = jnp.where(ahead, total[part] - prior[part] - hot[k], prior[part])
        count[k] = near + far

    g = iota((GRAMS, LANES), 0)
    col = iota((GRAMS, LANES), 1)
    d0 = sum(jnp.where(g >= 25 * m, 1, 0) for m in range(1, TOKENS))
    rest = g - 25 * d0
    d1 = sum(jnp.where(rest >= 5 * m, 1, 0) for m in range(1, TOKENS))
    d2 = rest - 5 * d1
    plain = g < 125
    d0 = jnp.where(plain, d0, NONE)
    d1 = jnp.where(plain, d1, NONE)
    d2 = jnp.where(plain, d2, NONE)
    d1 = jnp.where(g == 127, ids[0:1, 0:1], d1)
    d2 = jnp.where(g == 126, ids[0:1, 0:1], d2)
    d2 = jnp.where(g == 127, ids[0:1, 1:2], d2)
    d1 = jnp.where(g == 129, flip[ROWS - 1 :, LANES - 1 :], d1)
    d2 = jnp.where(g == 128, flip[ROWS - 1 :, LANES - 1 :], d2)
    d2 = jnp.where(g == 129, flip[ROWS - 1 :, LANES - 2 : LANES - 1], d2)
    tap = (col >> 3) % 3
    digit = jnp.where(tap == 0, d0, jnp.where(tap == 1, d1, d2))
    older[...] = jnp.where((digit == (col & 7)) & (col < 72), 1.0, 0.0).astype(bf16)

    place_row = iota((32, BLOCK), 0)
    lane_b = iota((BLOCK, BLOCK), 1)
    row_b = iota((BLOCK, BLOCK), 0)

    def own(x):
        first = jnp.sum(jnp.where(row == r0, x, 0), axis=0, keepdims=True)
        second = jnp.sum(jnp.where(row == r0 + 1, x, 0), axis=0, keepdims=True)
        return jnp.concatenate([first, second], axis=1)

    for s, values in enumerate((fs, rs)):
        digit = own(values[0])
        for k in range(3):
            digit = jnp.where(place_row < 8 * (3 - k), own(values[k + 1]), digit)
        hot_own = jnp.where(digit == (place_row & 7), 1.0, 0.0)
        now = hot_own[24:32]
        inclusive = (row_b <= lane_b) if s == 0 else (row_b >= lane_b)
        inclusive = jnp.where(inclusive, 1.0, 0.0).astype(bf16)
        counts = jnp.dot(now.astype(bf16), inclusive, preferred_element_type=f32)
        own_rows[16 * s : 16 * s + 8, :] = counts
        own_rows[16 * s + 8 : 16 * s + 16, :] = now
        hot_taps[s * BLOCK : (s + 1) * BLOCK, :] = jnp.concatenate(
            [hot_own] * 2 + [now] * 2 + [counts] * 3 + [jnp.zeros((24, BLOCK), f32)], axis=0
        ).T.astype(bf16)


def block_kernel(
    place, grams, side_tok, count, hot_taps, own_rows, older, t0, t1, t2, t3, vg, sq
):
    chunk = place[0] // 8
    r0 = place[0]
    tab = jnp.concatenate([t[0:32, :] for t in (t0, t1, t2, t3)], axis=1)
    dt_tab = tab[24:32]
    rate_tab = tab[7:8] * dt_tab * LOG2E
    log_tab = jnp.log2(jnp.maximum(dt_tab, TINY))
    pick = jnp.where(iota((HEADS, WIDE), 1) == HEAD * iota((HEADS, WIDE), 0), 1.0, 0.0).astype(bf16)

    def stack(*parts):
        return jnp.concatenate([part.astype(f32) for part in parts], axis=0).astype(bf16)

    spare = jnp.zeros((8, WIDE), f32)
    both_tab = stack(*split(rate_tab), *split(log_tab), spare, spare)
    both = lax.dot_general(pick, both_tab, NT, preferred_element_type=f32)
    rate = both[:, 0:8] + both[:, 8:16] + both[:, 16:24]
    log_dt = both[:, 24:32] + both[:, 32:40] + both[:, 40:48]
    both_t = lax.dot_general(both_tab, pick, NT, preferred_element_type=f32)
    rate_t = both_t[0:8] + both_t[8:16] + both_t[16:24]
    columns = [jnp.broadcast_to(-rate[:, k : k + 1], (HEADS, BLOCK)) for k in range(TOKENS)]

    def pair(ref, r):
        return jnp.concatenate([ref[pl.ds(r, 1), :], ref[pl.ds(r + 1, 1), :]], axis=1)

    nothing = jnp.zeros((HEADS, BLOCK), bf16)

    def weigh(r):
        token = jnp.broadcast_to(pair(side_tok, r), (HEADS, BLOCK)).astype(bf16)
        exponent = columns[0] * pair(count.at[0], r)
        for k in range(1, TOKENS):
            exponent = exponent + columns[k] * pair(count.at[k], r)
        weight = jnp.exp2(exponent)
        return token, weight

    def by_token(token, weight):
        return [jnp.where(token == k, weight, nothing) for k in range(TOKENS)]

    gram_row = iota((GRAMS, BLOCK), 0).astype(bf16)
    one = jnp.ones((GRAMS, BLOCK), bf16)
    none = jnp.zeros((GRAMS, BLOCK), bf16)

    def window(r):
        kind = jnp.broadcast_to(pair(grams, r), (GRAMS, BLOCK)).astype(bf16)
        return jnp.where(gram_row == kind, one, none)

    def tally(seen, weights):
        return lax.dot_general(
            jnp.concatenate(seen, axis=1),
            jnp.concatenate(weights, axis=1),
            NT,
            preferred_element_type=f32,
        )

    sides = [jnp.zeros((GRAMS, TOKENS * HEADS), f32) for _ in range(2)]
    for step in range(ROWS // 8):
        weights = []
        for j in range(4):
            token, weight = weigh(8 * step + 2 * j)
            weights.append(jnp.concatenate(by_token(token, weight.astype(bf16)), axis=0))
        part = tally([window(8 * step + 2 * j) for j in range(4)], weights)
        sides[0] = sides[0] + part * jnp.where(step < chunk, 1.0, 0.0)
        sides[1] = sides[1] + part * jnp.where(step > chunk, 1.0, 0.0)
    weights = []
    for j in range(4):
        r = pl.multiple_of(8 * chunk, 8) + 2 * j
        token, weight = weigh(r)
        first = jnp.where(r < r0, 1.0, 0.0)
        forward = by_token(token, (weight * first).astype(bf16))
        reverse = by_token(token, (weight * (1.0 - first)).astype(bf16))
        weights.append(jnp.concatenate(forward + reverse, axis=0))
    part = tally([window(pl.multiple_of(8 * chunk, 8) + 2 * j) for j in range(4)], weights)
    hist = (part + jnp.concatenate(sides, axis=1)).astype(bf16)

    taps = jnp.concatenate([tab[16 + k : 17 + k] * tab[8:16] for k in range(4)], axis=0)
    bc_taps = t0[32:64, :]
    kinds = older[...]
    rest = jnp.zeros((56, WIDE), f32)
    x_older = jnp.dot(kinds, stack(*split(taps[0:24]), rest), preferred_element_type=f32)
    b_older = jnp.dot(
        kinds, stack(*split(bc_taps[0:24, :STATE]), rest[:, :STATE]), preferred_element_type=f32
    )
    lift = iota((HEADS, WIDE), 1) - HEAD * iota((HEADS, WIDE), 0)
    lift = jnp.where((lift >= 0) & (lift < HEAD), 1.0, 0.0).astype(bf16)
    feeds = []
    moved = [[], []]
    for k in range(TOKENS):
        feeds.append(silu(b_older + bc_taps[24 + k : 25 + k, :STATE]).astype(bf16))
        act = (silu(x_older + taps[24 + k : 25 + k]) * dt_tab[k : k + 1]).astype(bf16)
        for s in range(2):
            start = (s * TOKENS + k) * HEADS
            part = jnp.dot(hist[:, start : start + HEADS], lift, preferred_element_type=f32)
            moved[s].append(act * part.astype(bf16))
    feeds = jnp.concatenate(feeds, axis=0)
    entering = [
        lax.dot_general(
            feeds, jnp.concatenate(moved[s], axis=0), TN, preferred_element_type=f32
        ).astype(bf16)
        for s in range(2)
    ]

    def look(hots, table):
        return jnp.dot(hots, table, preferred_element_type=f32)

    def blank(count, width):
        return jnp.zeros((count, width), f32)

    gate_tab = jnp.where(iota((8, WIDE), 0) < TOKENS, tab[0:8], 0.0)
    taps2 = stack(*split(taps, 2), blank(64, WIDE))
    bc2 = stack(*split(bc_taps, 2), blank(64, 2 * STATE))
    gate2 = stack(blank(64, WIDE), *split(gate_tab, 2), blank(48, WIDE))
    rate3 = stack(blank(80, HEADS), *split(rate_t), blank(24, HEADS))
    cap = jnp.broadcast_to(jnp.max(log_dt[:, :TOKENS], axis=1, keepdims=True), (HEADS, BLOCK))
    row_tab = jnp.concatenate([rate, log_dt], axis=1)
    lane_h = iota((LANES, LANES), 1)
    row_h = iota((LANES, LANES), 0)
    low = iota((BLOCK, LANES), 1) < HEAD
    zero = jnp.zeros((BLOCK, LANES), bf16)
    for s in range(2):
        rows = slice(s * BLOCK, (s + 1) * BLOCK)
        hot = hot_taps[rows, :]
        bc_act = silu(look(hot, bc2))
        feed = bc_act[:, :STATE].astype(bf16)
        read = bc_act[:, STATE:].astype(bf16)
        scores = lax.dot_general(read, feed, NT, preferred_element_type=f32)
        cum_row = -jnp.dot(
            row_tab, own_rows[16 * s : 16 * s + 16, :], precision=highest, preferred_element_type=f32
        )
        cum_col = -look(hot, rate3)
        decay = jnp.exp2(cum_col)
        near = (lane_h <= row_h) if s == 0 else (lane_h >= row_h)
        halves = ((0, 0, 1), (1, 0, 2)) if s == 0 else ((0, 0, 2), (1, 1, 1))
        masked = []
        for half, key, keys in halves:
            t = slice(half * LANES, (half + 1) * LANES)
            pieces = []
            for j in range(key, key + keys):
                piece = scores[t, j * LANES : (j + 1) * LANES]
                pieces.append(jnp.where(near, piece, 0.0) if j == half else piece)
            masked.append(jnp.concatenate(pieces, axis=1).astype(bf16))
        squares = [jnp.zeros((LANES, LANES), f32) for _ in range(2)]
        for p in range(HEADS // 2):
            chans = slice(p * LANES, (p + 1) * LANES)
            if p % 2 == 0:
                wide = slice(p * LANES, (p + 2) * LANES)
                xs_wide = silu(look(hot, taps2[:, wide]))
                gate_wide = look(hot, gate2[:, wide])
                far_wide = look(read, entering[s][:, wide])
            part = slice((p % 2) * LANES, (p % 2 + 1) * LANES)
            xs = xs_wide[:, part]
            gate = gate_wide[:, part]
            far = far_wide[:, part] * jnp.where(
                low, decay[:, 2 * p : 2 * p + 1], decay[:, 2 * p + 1 : 2 * p + 2]
            )
            fed = xs.astype(bf16)
            lows = jnp.where(low, fed, zero)
            highs = jnp.where(low, zero, fed)
            for (half, key, keys), score in zip(halves, masked):
                t = slice(half * LANES, (half + 1) * LANES)
                source = slice(key * LANES, (key + keys) * LANES)
                parts = []
                for h in (2 * p, 2 * p + 1):
                    differ = cum_col[t, h : h + 1] - cum_row[h : h + 1, source]
                    differ = jnp.minimum(differ, cap[h : h + 1, source])
                    parts.append(jnp.exp2(differ).astype(bf16) * score)
                y = jnp.dot(
                    jnp.concatenate(parts, axis=1),
                    jnp.concatenate([lows[source], highs[source]], axis=0),
                    preferred_element_type=f32,
                )
                v = (y + far[t] + tab[6:7, chans] * xs[t]) * gate[t]
                squares[half] = squares[half] + v * v
                out_rows = slice(s * BLOCK + half * LANES, s * BLOCK + (half + 1) * LANES)
                vg[out_rows, chans] = (v * tab[5:6, chans]).astype(bf16)
        summed = lax.dot_general(
            jnp.ones((8, LANES), f32),
            jnp.concatenate(squares, axis=0),
            NT,
            precision=highest,
            preferred_element_type=f32,
        )
        sq[:, rows] = summed[0:1]


def first_kernel(parity, vg, w_own, a1, a2, a3, forward, reverse, rest, known):
    half = LANES
    for s in range(2):
        rows = slice(s * BLOCK, (s + 1) * BLOCK)
        known[rows, 0 : 2 * half] = vg[rows, 0 : 2 * half]
        for d in range(3):
            even = vg[rows, (2 * d + 2) * half : (2 * d + 3) * half]
            odd = vg[rows, (2 * d + 3) * half : (2 * d + 4) * half]
            swapped = parity[0] == 1
            known[rows, (d + 2) * half : (d + 3) * half] = jnp.where(swapped, odd, even)
            rest[rows, d * half : (d + 1) * half] = jnp.where(swapped, even, odd)
    tile = 2 * LANES
    for n in range(forward.shape[1] // tile):
        cols = slice(n * tile, (n + 1) * tile)
        weights = jnp.concatenate([w[:, cols] for w in (w_own, a1, a2, a3)], axis=0)
        both = jnp.dot(known[...], weights, preferred_element_type=f32)
        forward[:, cols] = both[:BLOCK]
        reverse[:, cols] = both[BLOCK:]


def second_kernel(q0, q1, q2, q3, forward, reverse, rest, b1, b2, b3, out):
    first = iota((8, 2 * BLOCK), 0) == 0
    total = (q0[...] + q1[...]) + (q2[...] + q3[...])
    inverse = jnp.where(first, lax.rsqrt(total / 4096.0 + epsilon), 0.0)
    inverse = lax.dot_general(
        inverse, jnp.ones((8, LANES), f32), TN, precision=highest, preferred_element_type=f32
    )
    inverse = jnp.concatenate([inverse, inverse], axis=1)
    g = rest[...]
    tile = 2 * LANES
    for n in range(out.shape[0] // 2):
        cols = slice(n * tile, (n + 1) * tile)
        weights = jnp.concatenate([w[:, cols] for w in (b1, b2, b3)], axis=0)
        both = jnp.dot(g, weights, preferred_element_type=f32)
        result = (both[:BLOCK] + forward[:, cols]) * inverse[:BLOCK]
        result = (result + (both[BLOCK:] + reverse[:, cols]) * inverse[BLOCK:]).astype(bf16)
        out[2 * n] = result[:, :LANES]
        out[2 * n + 1] = result[:, LANES:]


def build_tables(
    parity, ids, count, w_out, embedding, norm_gain, w_z, w_x, w_bc, w_dt, dt_bias, a_log, d_skip, conv_x, conv_bc, gate_gain
):
    width = w_z.shape[1]
    given = (
        embedding,
        norm_gain[None],
        w_z,
        w_x,
        w_bc,
        w_dt.T,
        dt_bias[None],
        a_log[None],
        d_skip[None],
        conv_x,
        conv_bc,
        gate_gain[None],
    )
    return pl.pallas_call(
        table_kernel,
        in_specs=[pl.BlockSpec(memory_space=pltpu.SMEM), pl.BlockSpec(memory_space=pltpu.VMEM)]
        + [pl.BlockSpec(memory_space=pltpu.HBM)] * (TABLE_ARGS + 1),
        out_specs=(
            pl.BlockSpec(memory_space=pltpu.VMEM),
            pl.BlockSpec(memory_space=pltpu.VMEM),
            pl.BlockSpec(memory_space=pltpu.VMEM),
        ),
        out_shape=(
            jax.ShapeDtypeStruct((64, width), f32),
            jax.ShapeDtypeStruct((w_out.shape[0] // 2, w_out.shape[1]), w_out.dtype),
            jax.ShapeDtypeStruct((count, *ids.shape), i32),
        ),
        scratch_shapes=[pltpu.VMEM((8, embedding.shape[1]), f32)]
        + [pltpu.VMEM(x.shape, x.dtype) for x in given]
        + [pltpu.SemaphoreType.DMA((TABLE_ARGS + 3 * (PIECES - 1),)), pltpu.SemaphoreType.DMA(())],
        compiler_params=pltpu.CompilerParams(vmem_limit_bytes=60 * 2**20),
        name="tables",
    )(parity, ids, w_out, *given)


def prepare(place, complement, ids):
    smem = pl.BlockSpec(memory_space=pltpu.SMEM)
    vmem = pl.BlockSpec(memory_space=pltpu.VMEM)
    shape = jax.ShapeDtypeStruct
    return pl.pallas_call(
        prepare_kernel,
        in_specs=[smem, smem, vmem],
        out_specs=(vmem,) * 6,
        out_shape=(
            shape((ROWS, LANES), f32),
            shape((ROWS, LANES), f32),
            shape((TOKENS, ROWS, LANES), f32),
            shape((2 * BLOCK, LANES), bf16),
            shape((32, BLOCK), f32),
            shape((GRAMS, LANES), bf16),
        ),
        compiler_params=pltpu.CompilerParams(vmem_limit_bytes=32 * 2**20),
        name="prepare",
    )(place, complement, ids)


def run_block(place, prepared, tabs):
    smem = pl.BlockSpec(memory_space=pltpu.SMEM)
    vmem = pl.BlockSpec(memory_space=pltpu.VMEM)
    return pl.pallas_call(
        block_kernel,
        in_specs=[smem] + [vmem] * 10,
        out_specs=(vmem, vmem),
        out_shape=(
            jax.ShapeDtypeStruct((2 * BLOCK, WIDE), bf16),
            jax.ShapeDtypeStruct((1, 2 * BLOCK), f32),
        ),
        compiler_params=pltpu.CompilerParams(vmem_limit_bytes=48 * 2**20),
        cost_estimate=pl.CostEstimate(
            flops=40 * 10**9, bytes_accessed=100 * 2**20, transcendentals=10**7
        ),
        name="block",
    )(place, *prepared, *tabs)


def run_first(parity, vg, w_own, mine):
    features = w_own.shape[1]
    part = mine[0].shape[0]
    smem = pl.BlockSpec(memory_space=pltpu.SMEM)
    vmem = pl.BlockSpec(memory_space=pltpu.VMEM)
    return pl.pallas_call(
        first_kernel,
        in_specs=[smem] + [vmem] * 5,
        out_specs=(vmem,) * 3,
        out_shape=(
            jax.ShapeDtypeStruct((BLOCK, features), f32),
            jax.ShapeDtypeStruct((BLOCK, features), f32),
            jax.ShapeDtypeStruct((2 * BLOCK, 3 * part), bf16),
        ),
        scratch_shapes=[pltpu.VMEM((2 * BLOCK, 5 * part), bf16)],
        compiler_params=pltpu.CompilerParams(vmem_limit_bytes=32 * 2**20),
        cost_estimate=pl.CostEstimate(
            flops=60 * 10**9, bytes_accessed=100 * 2**20, transcendentals=0
        ),
        name="project_first",
    )(parity, vg, w_own, *mine)


def run_second(squares, forward, reverse, rest, theirs):
    features = forward.shape[1]
    vmem = pl.BlockSpec(memory_space=pltpu.VMEM)
    return pl.pallas_call(
        second_kernel,
        in_specs=[vmem] * 10,
        out_specs=vmem,
        out_shape=jax.ShapeDtypeStruct((features // LANES, BLOCK, LANES), bf16),
        compiler_params=pltpu.CompilerParams(vmem_limit_bytes=32 * 2**20),
        name="project_second",
    )(*squares, forward, reverse, rest, *theirs)


MATES = (
    [(t, (t + 8) % 16) for t in range(16)],
    [(t, ((t + 4) % 16) ^ 1) for t in range(16)],
    [(t, ((t - 4) % 16) ^ 1) for t in range(16)],
)


def exchange(x, group):
    return [lax.ppermute(x, "tensor", pairs) for pairs in group]


def other_core(x):
    count = lax.axis_size("context")
    return lax.ppermute(x, "context", [(i, i ^ 1) for i in range(count)])


def local(
    ids,
    complement,
    embedding,
    norm_gain,
    w_z,
    w_x,
    w_bc,
    w_dt,
    dt_bias,
    a_log,
    conv_x,
    conv_bc,
    d_skip,
    gate_gain,
    w_out,
):
    context = lax.axis_index("context").astype(i32)
    tensor = lax.axis_index("tensor").astype(i32)
    parity = context % 2
    quarter = (tensor // 2 + 2 * (tensor % 2) + 3) % 4
    place = (context * (ids.shape[0] // LANES) + quarter * (BLOCK // LANES)).reshape(1)
    tab, share, spread = build_tables(
        parity.reshape(1), ids.reshape(-1, LANES), lax.axis_size("context"), w_out,
        embedding, norm_gain, w_z, w_x, w_bc, w_dt, dt_bias, a_log, d_skip, conv_x, conv_bc, gate_gain
    )
    everyone = lax.all_to_all(spread, "context", 0, 0, tiled=True).reshape(ROWS, LANES)
    tabs = [tab] + exchange(tab, PEERS)
    everyone, tabs[1] = lax.optimization_barrier((everyone, tabs[1]))
    prepared = prepare(place, complement, everyone)
    mine = exchange(share, PEERS)

    vg, sq = run_block(place, prepared, tabs)
    squares = [sq] + exchange(sq, MATES)
    vg, *mine = lax.optimization_barrier((vg, *mine))
    theirs = [other_core(x) for x in mine]
    forward, reverse, rest = run_first(parity.reshape(1), vg, w_out, mine)
    terms = run_second(squares, forward, reverse, rest, theirs)
    arrived = lax.all_to_all(terms, "tensor", 0, 0, tiled=True)
    summed = [sum(arrived[t].astype(f32) for t in members) for members in QUARTERS]
    return jnp.concatenate(summed, axis=0).astype(bf16)


def solution(mesh):
    placed = (
        P("context"),
        P(),
        P(),
        P(),
        P(None, "tensor"),
        P(None, "tensor"),
        P(),
        P(None, "tensor"),
        P("tensor"),
        P("tensor"),
        P(None, "tensor"),
        P(),
        P("tensor"),
        P("tensor"),
        P("tensor", None),
    )
    return jax.shard_map(
        local, mesh=mesh, in_specs=placed, out_specs=P("context", "tensor"), check_vma=False
    )
```

```python
import functools

import jax
import jax.numpy as jnp
from jax import lax
from jax.experimental import pallas as pl
from jax.experimental.pallas import tpu as pltpu
from jax.sharding import PartitionSpec as P

f32 = jnp.float32
bf16 = jnp.bfloat16
i32 = jnp.int32
highest = lax.Precision.HIGHEST
epsilon = 1e-05

LANES = 128
SEQ = 16384
ROWS = SEQ // LANES
BLOCK = 256
STATE = 128
HEAD = 64
TOKENS = 5
NONE = 5
LOG2E = 1.4426950408889634
TINY = 2.0**-126
WIDE = 1024
HEADS = WIDE // HEAD
GRAMS = 144
TABLE_ARGS = 12
PIECES = 4

QUARTERS = [[t for t in range(16) if (t // 2 + 2 * (t % 2) + 3) % 4 == q] for q in range(4)]
PEERS = (
    [(t, (t + 2) % 16) for t in range(16)],
    [(t, (t - 2) % 16) for t in range(16)],
    [(t, t ^ 1) for t in range(16)],
)

TN = (((0,), (0,)), ((), ()))
NT = (((1,), (1,)), ((), ()))


def iota(shape, dim):
    return lax.broadcasted_iota(i32, shape, dim)


def silu(v):
    half = 0.5 * v
    return half + half * jnp.tanh(half)


def split(x, terms=3):
    parts = []
    for _ in range(terms):
        part = x.astype(bf16)
        parts.append(part)
        x = x - part.astype(f32)
    return parts


def table_kernel(parity, ids, w_out, *refs):
    given = refs[:TABLE_ARGS]
    tab, share, spread, rows = refs[TABLE_ARGS : TABLE_ARGS + 4]
    held = refs[TABLE_ARGS + 4 : -2]
    arrived, shared = refs[-2:]
    half = share.shape[0]
    part = w_out.at[pl.ds(pl.multiple_of(parity[0] * half, half), half), :]
    groups = []
    used = 0
    for source, target in zip(given, held):
        count = PIECES if source.shape[0] > 1024 else 1
        size = source.shape[0] // count
        group = []
        for n in range(count):
            span = pl.ds(n * size, size)
            one = (source, target) if count == 1 else (source.at[span, :], target.at[span, :])
            group.append(pltpu.make_async_copy(*one, arrived.at[used]))
            used += 1
        groups.append(group)
    for group in sorted(groups, key=len):
        for copy in group:
            copy.start()
    kept = pltpu.make_async_copy(part, share, shared)
    kept.start()
    spread[...] = jnp.broadcast_to(ids[...][None], spread.shape)
    for group in groups:
        if len(group) == 1:
            group[0].wait()
    emb, gain, wz, wx, wbc, wdt, bias, alog, dskip, convx, convbc, ggain = held
    rows[...] = jnp.zeros_like(rows)
    rows[0:TOKENS, :] = emb[...].astype(f32)
    e = rows[...]
    normed = (
        e * lax.rsqrt(jnp.mean(e * e, axis=-1, keepdims=True) + epsilon) * gain[...]
    ).astype(bf16)

    def project(w, group):
        for copy in group:
            copy.wait()
        return jnp.dot(normed, w[...], preferred_element_type=f32)

    z = project(wz, groups[2]).astype(bf16).astype(f32)
    xs = project(wx, groups[3]).astype(bf16).astype(f32)
    bc = project(wbc, groups[4]).astype(bf16).astype(f32)
    raw = lax.dot_general(normed, wdt[...], NT, preferred_element_type=f32) + bias[...]
    dt = jnp.maximum(raw, 0.0) + jnp.log1p(jnp.exp(-jnp.abs(raw)))
    width = z.shape[1]

    def spread(v):
        lane = iota((v.shape[0], width), 1)
        out = jnp.broadcast_to(v[:, 0:1], lane.shape)
        for h in range(1, v.shape[1]):
            out = jnp.where(lane >= h * HEAD, v[:, h : h + 1], out)
        return out

    row = iota((8, width), 0)
    own = jnp.where(row == 6, spread(dskip[...]), spread(jnp.exp(alog[...])))
    own = jnp.where(row == 5, ggain[...], own)
    tab[0:8, :] = jnp.where(row < TOKENS, silu(z), own)
    tab[8:16, :] = xs
    tab[16:24, :] = jnp.zeros((8, width), f32)
    tab[16:20, :] = convx[...]
    tab[24:32, :] = jnp.where(row < TOKENS, spread(dt), 0.0)
    for k in range(4):
        tab[32 + 8 * k : 40 + 8 * k, :] = convbc[k : k + 1, :] * bc
    kept.wait()


def prepare_kernel(
    place, comp, ids_ref, grams, side_tok, count, hot_taps, own_rows, older
):
    r0 = place[0]
    ids = ids_ref[...]
    row = iota((ROWS, LANES), 0)
    lane = iota((ROWS, LANES), 1)
    at = row * LANES + lane
    flip = jnp.zeros_like(ids)
    for k in range(TOKENS):
        flip = jnp.where(ids == k, comp[k], flip)

    def before(x):
        y = pltpu.roll(x, 1, 1)
        y = jnp.where(lane == 0, pltpu.roll(y, 1, 0), y)
        return jnp.where(at == 0, NONE, y)

    def after(x):
        y = pltpu.roll(x, LANES - 1, 1)
        y = jnp.where(lane == LANES - 1, pltpu.roll(y, ROWS - 1, 0), y)
        return jnp.where(at == SEQ - 1, NONE, y)

    fs = [ids]
    rs = [flip]
    for k in range(3):
        fs.append(before(fs[-1]))
        rs.append(after(rs[-1]))
    g_f = 25 * fs[3] + 5 * fs[2] + fs[1]
    g_r = 25 * rs[3] + 5 * rs[2] + rs[1]
    for k in range(3):
        g_f = jnp.where(at == k, 125 + k, g_f)
        g_r = jnp.where(at == SEQ - 1 - k, 125 if k == 0 else 127 + k, g_r)
    ahead = row < r0
    tok = jnp.where(ahead, ids, flip)
    tok = jnp.where(ahead | (row > r0 + 1), tok, -1)
    grams[...] = jnp.where(ahead, g_f, g_r).astype(f32)
    side_tok[...] = tok.astype(f32)

    hot = [jnp.where(tok == k, 1.0, 0.0) for k in range(TOKENS)]
    hots = jnp.concatenate(hot, axis=0).astype(bf16)
    strict = jnp.where(row < lane, 1.0, 0.0).astype(bf16)
    prior = jnp.dot(hots, strict, preferred_element_type=f32)
    total = jnp.dot(hots, jnp.ones((LANES, LANES), bf16), preferred_element_type=f32)
    between = ((row < lane) & (lane < r0)) | ((lane > r0 + 1) & (lane < row))
    between = jnp.where(between, 1.0, 0.0).astype(bf16)
    for k in range(TOKENS):
        part = slice(k * ROWS, (k + 1) * ROWS)
        far = jnp.dot(between, total[part].astype(bf16), preferred_element_type=f32)
        near = jnp.where(ahead, total[part] - prior[part] - hot[k], prior[part])
        count[k] = near + far

    g = iota((GRAMS, LANES), 0)
    col = iota((GRAMS, LANES), 1)
    d0 = sum(jnp.where(g >= 25 * m, 1, 0) for m in range(1, TOKENS))
    rest = g - 25 * d0
    d1 = sum(jnp.where(rest >= 5 * m, 1, 0) for m in range(1, TOKENS))
    d2 = rest - 5 * d1
    plain = g < 125
    d0 = jnp.where(plain, d0, NONE)
    d1 = jnp.where(plain, d1, NONE)
    d2 = jnp.where(plain, d2, NONE)
    d1 = jnp.where(g == 127, ids[0:1, 0:1], d1)
    d2 = jnp.where(g == 126, ids[0:1, 0:1], d2)
    d2 = jnp.where(g == 127, ids[0:1, 1:2], d2)
    d1 = jnp.where(g == 129, flip[ROWS - 1 :, LANES - 1 :], d1)
    d2 = jnp.where(g == 128, flip[ROWS - 1 :, LANES - 1 :], d2)
    d2 = jnp.where(g == 129, flip[ROWS - 1 :, LANES - 2 : LANES - 1], d2)
    tap = (col >> 3) % 3
    digit = jnp.where(tap == 0, d0, jnp.where(tap == 1, d1, d2))
    older[...] = jnp.where((digit == (col & 7)) & (col < 72), 1.0, 0.0).astype(bf16)

    place_row = iota((32, BLOCK), 0)
    lane_b = iota((BLOCK, BLOCK), 1)
    row_b = iota((BLOCK, BLOCK), 0)

    def own(x):
        first = jnp.sum(jnp.where(row == r0, x, 0), axis=0, keepdims=True)
        second = jnp.sum(jnp.where(row == r0 + 1, x, 0), axis=0, keepdims=True)
        return jnp.concatenate([first, second], axis=1)

    for s, values in enumerate((fs, rs)):
        digit = own(values[0])
        for k in range(3):
            digit = jnp.where(place_row < 8 * (3 - k), own(values[k + 1]), digit)
        hot_own = jnp.where(digit == (place_row & 7), 1.0, 0.0)
        now = hot_own[24:32]
        inclusive = (row_b <= lane_b) if s == 0 else (row_b >= lane_b)
        inclusive = jnp.where(inclusive, 1.0, 0.0).astype(bf16)
        counts = jnp.dot(now.astype(bf16), inclusive, preferred_element_type=f32)
        own_rows[16 * s : 16 * s + 8, :] = counts
        own_rows[16 * s + 8 : 16 * s + 16, :] = now
        hot_taps[s * BLOCK : (s + 1) * BLOCK, :] = jnp.concatenate(
            [hot_own] * 2 + [now] * 2 + [counts] * 3 + [jnp.zeros((24, BLOCK), f32)], axis=0
        ).T.astype(bf16)


def block_kernel(
    place, grams, side_tok, count, hot_taps, own_rows, older, t0, t1, t2, t3, vg, sq
):
    chunk = place[0] // 8
    r0 = place[0]
    tab = jnp.concatenate([t[0:32, :] for t in (t0, t1, t2, t3)], axis=1)
    dt_tab = tab[24:32]
    rate_tab = tab[7:8] * dt_tab * LOG2E
    log_tab = jnp.log2(jnp.maximum(dt_tab, TINY))
    pick = jnp.where(iota((HEADS, WIDE), 1) == HEAD * iota((HEADS, WIDE), 0), 1.0, 0.0).astype(bf16)

    def stack(*parts):
        return jnp.concatenate([part.astype(f32) for part in parts], axis=0).astype(bf16)

    spare = jnp.zeros((8, WIDE), f32)
    both_tab = stack(*split(rate_tab), *split(log_tab), spare, spare)
    both = lax.dot_general(pick, both_tab, NT, preferred_element_type=f32)
    rate = both[:, 0:8] + both[:, 8:16] + both[:, 16:24]
    log_dt = both[:, 24:32] + both[:, 32:40] + both[:, 40:48]
    both_t = lax.dot_general(both_tab, pick, NT, preferred_element_type=f32)
    rate_t = both_t[0:8] + both_t[8:16] + both_t[16:24]
    columns = [jnp.broadcast_to(-rate[:, k : k + 1], (HEADS, BLOCK)) for k in range(TOKENS)]

    def pair(ref, r):
        return jnp.concatenate([ref[pl.ds(r, 1), :], ref[pl.ds(r + 1, 1), :]], axis=1)

    nothing = jnp.zeros((HEADS, BLOCK), bf16)

    def weigh(r):
        token = jnp.broadcast_to(pair(side_tok, r), (HEADS, BLOCK)).astype(bf16)
        exponent = columns[0] * pair(count.at[0], r)
        for k in range(1, TOKENS):
            exponent = exponent + columns[k] * pair(count.at[k], r)
        weight = jnp.exp2(exponent)
        return token, weight

    def by_token(token, weight):
        return [jnp.where(token == k, weight, nothing) for k in range(TOKENS)]

    gram_row = iota((GRAMS, BLOCK), 0).astype(bf16)
    one = jnp.ones((GRAMS, BLOCK), bf16)
    none = jnp.zeros((GRAMS, BLOCK), bf16)

    def window(r):
        kind = jnp.broadcast_to(pair(grams, r), (GRAMS, BLOCK)).astype(bf16)
        return jnp.where(gram_row == kind, one, none)

    def tally(seen, weights):
        return lax.dot_general(
            jnp.concatenate(seen, axis=1),
            jnp.concatenate(weights, axis=1),
            NT,
            preferred_element_type=f32,
        )

    sides = [jnp.zeros((GRAMS, TOKENS * HEADS), f32) for _ in range(2)]
    for step in range(ROWS // 8):
        weights = []
        for j in range(4):
            token, weight = weigh(8 * step + 2 * j)
            weights.append(jnp.concatenate(by_token(token, weight.astype(bf16)), axis=0))
        part = tally([window(8 * step + 2 * j) for j in range(4)], weights)
        sides[0] = sides[0] + part * jnp.where(step < chunk, 1.0, 0.0)
        sides[1] = sides[1] + part * jnp.where(step > chunk, 1.0, 0.0)
    weights = []
    for j in range(4):
        r = pl.multiple_of(8 * chunk, 8) + 2 * j
        token, weight = weigh(r)
        first = jnp.where(r < r0, 1.0, 0.0)
        forward = by_token(token, (weight * first).astype(bf16))
        reverse = by_token(token, (weight * (1.0 - first)).astype(bf16))
        weights.append(jnp.concatenate(forward + reverse, axis=0))
    part = tally([window(pl.multiple_of(8 * chunk, 8) + 2 * j) for j in range(4)], weights)
    hist = (part + jnp.concatenate(sides, axis=1)).astype(bf16)

    taps = jnp.concatenate([tab[16 + k : 17 + k] * tab[8:16] for k in range(4)], axis=0)
    bc_taps = t0[32:64, :]
    kinds = older[...]
    rest = jnp.zeros((56, WIDE), f32)
    x_older = jnp.dot(kinds, stack(*split(taps[0:24]), rest), preferred_element_type=f32)
    b_older = jnp.dot(
        kinds, stack(*split(bc_taps[0:24, :STATE]), rest[:, :STATE]), preferred_element_type=f32
    )
    lift = iota((HEADS, WIDE), 1) - HEAD * iota((HEADS, WIDE), 0)
    lift = jnp.where((lift >= 0) & (lift < HEAD), 1.0, 0.0).astype(bf16)
    feeds = []
    moved = [[], []]
    for k in range(TOKENS):
        feeds.append(silu(b_older + bc_taps[24 + k : 25 + k, :STATE]).astype(bf16))
        act = (silu(x_older + taps[24 + k : 25 + k]) * dt_tab[k : k + 1]).astype(bf16)
        for s in range(2):
            start = (s * TOKENS + k) * HEADS
            part = jnp.dot(hist[:, start : start + HEADS], lift, preferred_element_type=f32)
            moved[s].append(act * part.astype(bf16))
    feeds = jnp.concatenate(feeds, axis=0)
    entering = [
        lax.dot_general(
            feeds, jnp.concatenate(moved[s], axis=0), TN, preferred_element_type=f32
        ).astype(bf16)
        for s in range(2)
    ]

    def look(hots, table):
        return jnp.dot(hots, table, preferred_element_type=f32)

    def blank(count, width):
        return jnp.zeros((count, width), f32)

    gate_tab = jnp.where(iota((8, WIDE), 0) < TOKENS, tab[0:8], 0.0)
    taps2 = stack(*split(taps, 2), blank(64, WIDE))
    bc2 = stack(*split(bc_taps, 2), blank(64, 2 * STATE))
    gate2 = stack(blank(64, WIDE), *split(gate_tab, 2), blank(48, WIDE))
    rate3 = stack(blank(80, HEADS), *split(rate_t), blank(24, HEADS))
    cap = jnp.broadcast_to(jnp.max(log_dt[:, :TOKENS], axis=1, keepdims=True), (HEADS, BLOCK))
    row_tab = jnp.concatenate([rate, log_dt], axis=1)
    lane_h = iota((LANES, LANES), 1)
    row_h = iota((LANES, LANES), 0)
    low = iota((BLOCK, LANES), 1) < HEAD
    zero = jnp.zeros((BLOCK, LANES), bf16)
    for s in range(2):
        rows = slice(s * BLOCK, (s + 1) * BLOCK)
        hot = hot_taps[rows, :]
        bc_act = silu(look(hot, bc2))
        feed = bc_act[:, :STATE].astype(bf16)
        read = bc_act[:, STATE:].astype(bf16)
        scores = lax.dot_general(read, feed, NT, preferred_element_type=f32)
        cum_row = -jnp.dot(
            row_tab, own_rows[16 * s : 16 * s + 16, :], precision=highest, preferred_element_type=f32
        )
        cum_col = -look(hot, rate3)
        decay = jnp.exp2(cum_col)
        near = (lane_h <= row_h) if s == 0 else (lane_h >= row_h)
        halves = ((0, 0, 1), (1, 0, 2)) if s == 0 else ((0, 0, 2), (1, 1, 1))
        masked = []
        for half, key, keys in halves:
            t = slice(half * LANES, (half + 1) * LANES)
            pieces = []
            for j in range(key, key + keys):
                piece = scores[t, j * LANES : (j + 1) * LANES]
                pieces.append(jnp.where(near, piece, 0.0) if j == half else piece)
            masked.append(jnp.concatenate(pieces, axis=1).astype(bf16))
        squares = [jnp.zeros((LANES, LANES), f32) for _ in range(2)]
        for p in range(HEADS // 2):
            chans = slice(p * LANES, (p + 1) * LANES)
            if p % 2 == 0:
                wide = slice(p * LANES, (p + 2) * LANES)
                xs_wide = silu(look(hot, taps2[:, wide]))
                gate_wide = look(hot, gate2[:, wide])
                far_wide = look(read, entering[s][:, wide])
            part = slice((p % 2) * LANES, (p % 2 + 1) * LANES)
            xs = xs_wide[:, part]
            gate = gate_wide[:, part]
            far = far_wide[:, part] * jnp.where(
                low, decay[:, 2 * p : 2 * p + 1], decay[:, 2 * p + 1 : 2 * p + 2]
            )
            fed = xs.astype(bf16)
            lows = jnp.where(low, fed, zero)
            highs = jnp.where(low, zero, fed)
            for (half, key, keys), score in zip(halves, masked):
                t = slice(half * LANES, (half + 1) * LANES)
                source = slice(key * LANES, (key + keys) * LANES)
                parts = []
                for h in (2 * p, 2 * p + 1):
                    differ = cum_col[t, h : h + 1] - cum_row[h : h + 1, source]
                    differ = jnp.minimum(differ, cap[h : h + 1, source])
                    parts.append(jnp.exp2(differ).astype(bf16) * score)
                y = jnp.dot(
                    jnp.concatenate(parts, axis=1),
                    jnp.concatenate([lows[source], highs[source]], axis=0),
                    preferred_element_type=f32,
                )
                v = (y + far[t] + tab[6:7, chans] * xs[t]) * gate[t]
                squares[half] = squares[half] + v * v
                out_rows = slice(s * BLOCK + half * LANES, s * BLOCK + (half + 1) * LANES)
                vg[out_rows, chans] = (v * tab[5:6, chans]).astype(bf16)
        summed = lax.dot_general(
            jnp.ones((8, LANES), f32),
            jnp.concatenate(squares, axis=0),
            NT,
            precision=highest,
            preferred_element_type=f32,
        )
        sq[:, rows] = summed[0:1]


def first_kernel(parity, vg, w_own, a1, a2, a3, forward, reverse, rest, known):
    half = LANES
    for s in range(2):
        rows = slice(s * BLOCK, (s + 1) * BLOCK)
        known[rows, 0 : 2 * half] = vg[rows, 0 : 2 * half]
        for d in range(3):
            even = vg[rows, (2 * d + 2) * half : (2 * d + 3) * half]
            odd = vg[rows, (2 * d + 3) * half : (2 * d + 4) * half]
            swapped = parity[0] == 1
            known[rows, (d + 2) * half : (d + 3) * half] = jnp.where(swapped, odd, even)
            rest[rows, d * half : (d + 1) * half] = jnp.where(swapped, even, odd)
    tile = 2 * LANES
    for n in range(forward.shape[1] // tile):
        cols = slice(n * tile, (n + 1) * tile)
        weights = jnp.concatenate([w[:, cols] for w in (w_own, a1, a2, a3)], axis=0)
        both = jnp.dot(known[...], weights, preferred_element_type=f32)
        forward[:, cols] = both[:BLOCK]
        reverse[:, cols] = both[BLOCK:]


def second_kernel(q0, q1, q2, q3, forward, reverse, rest, b1, b2, b3, out):
    first = iota((8, 2 * BLOCK), 0) == 0
    total = (q0[...] + q1[...]) + (q2[...] + q3[...])
    inverse = jnp.where(first, lax.rsqrt(total / 4096.0 + epsilon), 0.0)
    inverse = lax.dot_general(
        inverse, jnp.ones((8, LANES), f32), TN, precision=highest, preferred_element_type=f32
    )
    inverse = jnp.concatenate([inverse, inverse], axis=1)
    g = rest[...]
    tile = 2 * LANES
    for n in range(out.shape[0] // 2):
        cols = slice(n * tile, (n + 1) * tile)
        weights = jnp.concatenate([w[:, cols] for w in (b1, b2, b3)], axis=0)
        both = jnp.dot(g, weights, preferred_element_type=f32)
        result = (both[:BLOCK] + forward[:, cols]) * inverse[:BLOCK]
        result = (result + (both[BLOCK:] + reverse[:, cols]) * inverse[BLOCK:]).astype(bf16)
        out[2 * n] = result[:, :LANES]
        out[2 * n + 1] = result[:, LANES:]


def build_tables(
    parity, ids, count, w_out, embedding, norm_gain, w_z, w_x, w_bc, w_dt, dt_bias, a_log, d_skip, conv_x, conv_bc, gate_gain
):
    width = w_z.shape[1]
    given = (
        embedding,
        norm_gain[None],
        w_z,
        w_x,
        w_bc,
        w_dt.T,
        dt_bias[None],
        a_log[None],
        d_skip[None],
        conv_x,
        conv_bc,
        gate_gain[None],
    )
    return pl.pallas_call(
        table_kernel,
        in_specs=[pl.BlockSpec(memory_space=pltpu.SMEM), pl.BlockSpec(memory_space=pltpu.VMEM)]
        + [pl.BlockSpec(memory_space=pltpu.HBM)] * (TABLE_ARGS + 1),
        out_specs=(
            pl.BlockSpec(memory_space=pltpu.VMEM),
            pl.BlockSpec(memory_space=pltpu.VMEM),
            pl.BlockSpec(memory_space=pltpu.VMEM),
        ),
        out_shape=(
            jax.ShapeDtypeStruct((64, width), f32),
            jax.ShapeDtypeStruct((w_out.shape[0] // 2, w_out.shape[1]), w_out.dtype),
            jax.ShapeDtypeStruct((count, *ids.shape), i32),
        ),
        scratch_shapes=[pltpu.VMEM((8, embedding.shape[1]), f32)]
        + [pltpu.VMEM(x.shape, x.dtype) for x in given]
        + [pltpu.SemaphoreType.DMA((TABLE_ARGS + 3 * (PIECES - 1),)), pltpu.SemaphoreType.DMA(())],
        compiler_params=pltpu.CompilerParams(vmem_limit_bytes=60 * 2**20),
        name="tables",
    )(parity, ids, w_out, *given)


def prepare(place, complement, ids):
    smem = pl.BlockSpec(memory_space=pltpu.SMEM)
    vmem = pl.BlockSpec(memory_space=pltpu.VMEM)
    shape = jax.ShapeDtypeStruct
    return pl.pallas_call(
        prepare_kernel,
        in_specs=[smem, smem, vmem],
        out_specs=(vmem,) * 6,
        out_shape=(
            shape((ROWS, LANES), f32),
            shape((ROWS, LANES), f32),
            shape((TOKENS, ROWS, LANES), f32),
            shape((2 * BLOCK, LANES), bf16),
            shape((32, BLOCK), f32),
            shape((GRAMS, LANES), bf16),
        ),
        compiler_params=pltpu.CompilerParams(vmem_limit_bytes=32 * 2**20),
        name="prepare",
    )(place, complement, ids)


def run_block(place, prepared, tabs):
    smem = pl.BlockSpec(memory_space=pltpu.SMEM)
    vmem = pl.BlockSpec(memory_space=pltpu.VMEM)
    return pl.pallas_call(
        block_kernel,
        in_specs=[smem] + [vmem] * 10,
        out_specs=(vmem, vmem),
        out_shape=(
            jax.ShapeDtypeStruct((2 * BLOCK, WIDE), bf16),
            jax.ShapeDtypeStruct((1, 2 * BLOCK), f32),
        ),
        compiler_params=pltpu.CompilerParams(vmem_limit_bytes=48 * 2**20),
        cost_estimate=pl.CostEstimate(
            flops=40 * 10**9, bytes_accessed=100 * 2**20, transcendentals=10**7
        ),
        name="block",
    )(place, *prepared, *tabs)


def run_first(parity, vg, w_own, mine):
    features = w_own.shape[1]
    part = mine[0].shape[0]
    smem = pl.BlockSpec(memory_space=pltpu.SMEM)
    vmem = pl.BlockSpec(memory_space=pltpu.VMEM)
    return pl.pallas_call(
        first_kernel,
        in_specs=[smem] + [vmem] * 5,
        out_specs=(vmem,) * 3,
        out_shape=(
            jax.ShapeDtypeStruct((BLOCK, features), f32),
            jax.ShapeDtypeStruct((BLOCK, features), f32),
            jax.ShapeDtypeStruct((2 * BLOCK, 3 * part), bf16),
        ),
        scratch_shapes=[pltpu.VMEM((2 * BLOCK, 5 * part), bf16)],
        compiler_params=pltpu.CompilerParams(vmem_limit_bytes=32 * 2**20),
        cost_estimate=pl.CostEstimate(
            flops=60 * 10**9, bytes_accessed=100 * 2**20, transcendentals=0
        ),
        name="project_first",
    )(parity, vg, w_own, *mine)


def run_second(squares, forward, reverse, rest, theirs):
    features = forward.shape[1]
    vmem = pl.BlockSpec(memory_space=pltpu.VMEM)
    return pl.pallas_call(
        second_kernel,
        in_specs=[vmem] * 10,
        out_specs=vmem,
        out_shape=jax.ShapeDtypeStruct((features // LANES, BLOCK, LANES), bf16),
        compiler_params=pltpu.CompilerParams(vmem_limit_bytes=32 * 2**20),
        name="project_second",
    )(*squares, forward, reverse, rest, *theirs)


MATES = (
    [(t, (t + 8) % 16) for t in range(16)],
    [(t, ((t + 4) % 16) ^ 1) for t in range(16)],
    [(t, ((t - 4) % 16) ^ 1) for t in range(16)],
)


def exchange(x, group):
    return [lax.ppermute(x, "tensor", pairs) for pairs in group]


def other_core(x):
    count = lax.axis_size("context")
    return lax.ppermute(x, "context", [(i, i ^ 1) for i in range(count)])


def local(
    ids,
    complement,
    embedding,
    norm_gain,
    w_z,
    w_x,
    w_bc,
    w_dt,
    dt_bias,
    a_log,
    conv_x,
    conv_bc,
    d_skip,
    gate_gain,
    w_out,
):
    context = lax.axis_index("context").astype(i32)
    tensor = lax.axis_index("tensor").astype(i32)
    parity = context % 2
    quarter = (tensor // 2 + 2 * (tensor % 2) + 3) % 4
    place = (context * (ids.shape[0] // LANES) + quarter * (BLOCK // LANES)).reshape(1)
    tab, share, spread = build_tables(
        parity.reshape(1), ids.reshape(-1, LANES), lax.axis_size("context"), w_out,
        embedding, norm_gain, w_z, w_x, w_bc, w_dt, dt_bias, a_log, d_skip, conv_x, conv_bc, gate_gain
    )
    everyone = lax.all_to_all(spread, "context", 0, 0, tiled=True).reshape(ROWS, LANES)
    tabs = [tab] + exchange(tab, PEERS)
    prepared = prepare(place, complement, everyone)
    mine = exchange(share, PEERS)

    vg, sq = run_block(place, prepared, tabs)
    squares = [sq] + exchange(sq, MATES)
    vg, *mine = lax.optimization_barrier((vg, *mine))
    theirs = [other_core(x) for x in mine]
    forward, reverse, rest = run_first(parity.reshape(1), vg, w_out, mine)
    terms = run_second(squares, forward, reverse, rest, theirs)
    arrived = lax.all_to_all(terms, "tensor", 0, 0, tiled=True)
    summed = [sum(arrived[t].astype(f32) for t in members) for members in QUARTERS]
    return jnp.concatenate(summed, axis=0).astype(bf16)


def solution(mesh):
    placed = (
        P("context"),
        P(),
        P(),
        P(),
        P(None, "tensor"),
        P(None, "tensor"),
        P(),
        P(None, "tensor"),
        P("tensor"),
        P("tensor"),
        P(None, "tensor"),
        P(),
        P("tensor"),
        P("tensor"),
        P("tensor", None),
    )
    return jax.shard_map(
        local, mesh=mesh, in_specs=placed, out_specs=P("context", "tensor"), check_vma=False
    )
```
